512 devices in a mesh: lon: 32 (over x, y, z_hi), lat: 16 (over z_lo, core).
Axes of the slice: x: 4, y: 4, z: 16 (z_hi: 2, z_lo: 8; z = z_hi * 8 + z_lo), core: 2. Of those that a mesh axis runs over, the one named last changes fastest.
Arguments:
- tokens: bfloat16 [4, 192, 384, 512], P(None, 'lat', 'lon'), may hold values from -6 to 6
- gain_attn: float32 [512], replicated, may hold values from 0.1 to 1.9
- weight_qkv: bfloat16 [512, 1536], replicated, may hold values from -0.25 to 0.25
- weight_out: bfloat16 [512, 512], replicated, may hold values from -0.25 to 0.25
Outputs:
- mixed: bfloat16 [4, 192, 384, 512], P(None, 'lat', 'lon')
The draws below stay inside these ranges and needn't reach their ends.
All inputs are finite; a program needn't handle non-finite values.
Results may differ from the reference program's by a relative error of at most 0.0043.
Values may be sent and summed in bfloat16 or wider, within the bound.
No kernel may reach another device: no remote copies, remote signals or barrier semaphores. Data moves between devices by JAX's collectives and lax.ppermute only.
A program may use at most 128 MiB of HBM per device.

```python
import jax
import jax.numpy as jnp
from jax import lax

D = 512
HEADS = 8
HEAD_SIZE = 64
LEV = 4
WIN_LEV = 2
WIN_LAT = 6
WIN_LON = 12
SHIFT_LEV = 1
SHIFT_LAT = 3
SHIFT_LON = 6
NLAT = 192
NLON = 384


def level_of(own_key, shape, cuts, smallest, largest):
    loudness = 1.0
    for position, blocks in cuts:
        steps = jax.random.uniform(jax.random.fold_in(jax.random.fold_in(own_key, 6), position), (blocks,), jnp.float32, smallest / len(cuts), largest / len(cuts))
        loudness = loudness * jnp.repeat(jnp.exp(steps), shape[position] // blocks).reshape((-1,) + (1,) * (len(shape) - 1 - position))
    return loudness


def noise(own_key, dims, scale, most, cuts=(), held_as=jnp.bfloat16):
    level = level_of(own_key, dims, cuts, -0.22, 0.18) if cuts else 1.0
    values = jax.random.normal(own_key, dims, jnp.float32) * scale * level
    return jnp.minimum(jnp.maximum(values, -most), most).astype(held_as)


def setup_inputs(seed: int = 0) -> dict:
    key_list = jax.random.split(jax.random.key(seed), 5)
    tokens = noise(key_list[0], (LEV, NLAT, NLON, D), 1.0, 6.0, ((1, 16), (2, 32)))
    gain_attn = jnp.clip(1.0 + 0.18 * jax.random.normal(key_list[1], (D,), jnp.float32), 0.1, 1.9)
    weight_qkv = noise(key_list[2], (D, 3 * D), D ** -0.5, 0.25)
    weight_out = noise(key_list[3], (D, D), D ** -0.5, 0.25)
    return dict(tokens=tokens, gain_attn=gain_attn, weight_qkv=weight_qkv, weight_out=weight_out)


EPS = 1e-05

def layer_norm(values, gain):
    center = values - lax.optimization_barrier(jnp.mean(values, axis=-1, keepdims=True))
    spread = lax.optimization_barrier(jnp.mean(center * center, axis=-1, keepdims=True))
    return center * lax.rsqrt(spread + EPS) * gain

def region_ids(lev_count, lat_rows, lat_total):
    levels = jnp.arange(lev_count, dtype=jnp.int32)
    lev_part = jnp.where(levels < lev_count - WIN_LEV, 0, jnp.where(levels < lev_count - SHIFT_LEV, 1, 2))
    lat_part = jnp.where(lat_rows < lat_total - WIN_LAT, 0, jnp.where(lat_rows < lat_total - SHIFT_LAT, 1, 2))
    return (lev_part[:, None] * 3 + lat_part[None, :]).astype(jnp.int32)

def to_windows(grid):
    lev_count, row_count, col_count, chans = grid.shape
    split = grid.reshape(lev_count // WIN_LEV, WIN_LEV, row_count // WIN_LAT, WIN_LAT, col_count // WIN_LON, WIN_LON, chans)
    return split.transpose(0, 2, 4, 1, 3, 5, 6).reshape(-1, WIN_LEV * WIN_LAT * WIN_LON, chans)

def from_windows(windows, lev_count, row_count, col_count):
    chans = windows.shape[-1]
    split = windows.reshape(lev_count // WIN_LEV, row_count // WIN_LAT, col_count // WIN_LON, WIN_LEV, WIN_LAT, WIN_LON, chans)
    return split.transpose(0, 3, 1, 4, 2, 5, 6).reshape(lev_count, row_count, col_count, chans)

def attend(shifted, region, gain_attn, weight_qkv, weight_out):
    lev_count, row_count, col_count, feat_width = shifted.shape
    normed = layer_norm(shifted.astype(jnp.float32), gain_attn).astype(jnp.bfloat16)
    packed = jnp.dot(normed.reshape(-1, feat_width), weight_qkv, preferred_element_type=jnp.float32).astype(jnp.bfloat16)
    windows = to_windows(packed.reshape(lev_count, row_count, col_count, 3 * feat_width))
    win_count, span = (windows.shape[0], windows.shape[1])
    windows = windows.reshape(win_count, span, 3, HEADS, HEAD_SIZE)
    query, keys, values_in = (windows[:, :, 0], windows[:, :, 1], windows[:, :, 2])
    scores = jnp.einsum('wqhe,wkhe->whqk', query.astype(jnp.float32), keys.astype(jnp.float32)) * HEAD_SIZE ** (-0.5)
    labels = to_windows(jnp.broadcast_to(region[:, :, None, None], (lev_count, row_count, col_count, 1)))[:, :, 0]
    same = (labels[:, :, None] == labels[:, None, :])[:, None]
    expo = jnp.where(same, jnp.exp(scores), jnp.float32(0.0))
    attn_probs = (expo / lax.optimization_barrier(jnp.sum(expo, axis=-1, keepdims=True))).astype(jnp.bfloat16)
    heads_out = jnp.einsum('whqk,wkhe->wqhe', attn_probs.astype(jnp.float32), values_in.astype(jnp.float32)).astype(jnp.bfloat16)
    merged = from_windows(heads_out.reshape(win_count, span, feat_width), lev_count, row_count, col_count)
    projected = jnp.dot(merged.reshape(-1, feat_width), weight_out, preferred_element_type=jnp.float32)
    return projected.astype(jnp.bfloat16).reshape(shifted.shape)

def reference(tokens, gain_attn, weight_qkv, weight_out):
    shifted = jnp.roll(tokens, (-SHIFT_LEV, -SHIFT_LAT, -SHIFT_LON), axis=(0, 1, 2))

    def band(band_index):
        start = band_index * WIN_LAT
        piece = lax.dynamic_slice_in_dim(shifted, start, WIN_LAT, 1)
        lat_rows = (start + jnp.arange(WIN_LAT, dtype=jnp.int32)).astype(jnp.int32)
        region = region_ids(LEV, lat_rows, NLAT)
        return attend(piece, region, gain_attn, weight_qkv, weight_out)
    bands = lax.map(band, jnp.arange(NLAT // WIN_LAT, dtype=jnp.int32))
    attn_out = jnp.transpose(bands, (1, 0, 2, 3, 4)).reshape(LEV, NLAT, NLON, D)
    attn_out = jnp.roll(attn_out, (SHIFT_LEV, SHIFT_LAT, SHIFT_LON), axis=(0, 1, 2))
    return (tokens.astype(jnp.float32) + attn_out.astype(jnp.float32)).astype(jnp.bfloat16)
```

```python
import jax
import jax.numpy as jnp
from jax import lax
from jax.experimental import pallas as pl
from jax.experimental.pallas import tpu as pltpu
from jax.sharding import PartitionSpec as P

HEADS = 8
HEAD_SIZE = 64
GROUP = 4
EPS = 1e-05
FAR = -1e30
HALF = 6
EDGE = 3


def shift(value, axis, by, wrap):
    count = lax.axis_size(axis)
    pairs = [(i, (i + by) % count) for i in range(count) if wrap or 0 <= i + by < count]
    return lax.ppermute(value, axis, pairs)


def layer_norm(values, gain):
    center = values - jnp.mean(values, axis=-1, keepdims=True)
    spread = jnp.mean(center * center, axis=-1, keepdims=True)
    return (center * lax.rsqrt(spread + EPS) * gain).astype(jnp.bfloat16)


def matmul(a, b):
    return jnp.dot(a, b, preferred_element_type=jnp.float32)


def attend(query, keys, values, bias):
    rows = query.shape[0]
    span = GROUP * HEAD_SIZE
    owner = lax.broadcasted_iota(jnp.int32, (rows, span), 1) // HEAD_SIZE
    tall = jnp.concatenate([bias] * GROUP, axis=0)
    parts = []
    for start in range(0, query.shape[1], span):
        piece = query[:, start : start + span]
        spread = jnp.concatenate(
            [jnp.where(owner == h, piece, 0.0) for h in range(GROUP)], axis=0
        ).astype(jnp.bfloat16)
        scores = lax.dot_general(
            spread,
            keys[:, start : start + span],
            (((1,), (1,)), ((), ())),
            preferred_element_type=jnp.float32,
        )
        scores = scores + tall
        expo = jnp.exp(scores - jnp.max(scores, axis=-1, keepdims=True))
        total = jnp.sum(expo, axis=-1, keepdims=True)
        out = matmul(expo.astype(jnp.bfloat16), values[:, start : start + span]) / total
        merged = jnp.zeros((rows, span), jnp.float32)
        for h in range(GROUP):
            merged = jnp.where(owner == h, out[h * rows : (h + 1) * rows], merged)
        parts.append(merged)
    return jnp.concatenate(parts, axis=1).astype(jnp.bfloat16)


def project(tokens, heads, weight_ref):
    branch = matmul(heads, weight_ref[...]).astype(jnp.bfloat16)
    return (tokens + branch.astype(jnp.float32)).astype(jnp.bfloat16)


def inner_kernel(own_ref, west_ref, east_ref, bias_ref, gain_ref, qkv_ref, out_w_ref, out_ref):
    width = own_ref.shape[-1]
    lo = EDGE * HALF * 4
    hi = own_ref.shape[1] - lo
    own = own_ref[...].astype(jnp.float32)
    halos = [west_ref[...].astype(jnp.float32), east_ref[...].astype(jnp.float32)]
    tokens = jnp.concatenate([own[0, lo:hi], own[1, lo:hi]], axis=0)
    count = hi - lo
    gain = gain_ref[...]
    mine = layer_norm(tokens, gain)
    theirs = layer_norm(jnp.concatenate([h[lo:hi] for h in halos], axis=0), gain)
    query = matmul(mine, qkv_ref[:, :width]).astype(jnp.bfloat16).astype(jnp.float32) * HEAD_SIZE**-0.5
    mine_kv = matmul(mine, qkv_ref[:, width:]).astype(jnp.bfloat16)
    their_kv = matmul(theirs, qkv_ref[:, width:]).astype(jnp.bfloat16)
    heads = []
    for side in range(2):
        at = slice(side * count, (side + 1) * count)
        both = jnp.concatenate([mine_kv[at], their_kv[at]], axis=0)
        heads.append(attend(query[at], both[:, :width], both[:, width:], bias_ref[...]))
    out_ref[...] = project(tokens, jnp.concatenate(heads, axis=0), out_w_ref)


def edge_kernel(own_ref, west_ref, east_ref, lat_ref, far_ref, bias_ref, gain_ref, qkv_ref, out_w_ref, out_ref):
    width = own_ref.shape[-1]
    count = EDGE * HALF * 4
    size = own_ref.shape[1]
    own = own_ref[...].astype(jnp.float32)
    halos = [west_ref[...].astype(jnp.float32), east_ref[...].astype(jnp.float32)]
    gain = gain_ref[...]
    tokens, heads = [], []
    for edge in range(2):
        at = slice(0, count) if edge == 0 else slice(size - count, size)
        for side in range(2):
            mine = own[side, at]
            tokens.append(mine)
            window = jnp.concatenate(
                [
                    mine,
                    halos[side][at],
                    lat_ref[edge, side].astype(jnp.float32),
                    far_ref[edge, side].astype(jnp.float32),
                ],
                axis=0,
            )
            normed = layer_norm(window, gain)
            query = matmul(normed, qkv_ref[:, :width])[:count]
            query = query.astype(jnp.bfloat16).astype(jnp.float32) * HEAD_SIZE**-0.5
            kv = matmul(normed, qkv_ref[:, width:]).astype(jnp.bfloat16)
            heads.append(attend(query, kv[:, :width], kv[:, width:], bias_ref[edge]))
    tokens = jnp.concatenate(tokens, axis=0)
    heads = jnp.concatenate([h.astype(jnp.float32) for h in heads], axis=0).astype(jnp.bfloat16)
    out_ref[...] = project(tokens, heads, out_w_ref)


def call(kernel, rows, flops, *operands):
    width = operands[0].shape[-1]
    moved = sum(x.size * x.dtype.itemsize for x in operands) + rows * width * 2
    vmem = pl.BlockSpec(memory_space=pltpu.VMEM)
    return pl.pallas_call(
        kernel,
        out_shape=jax.ShapeDtypeStruct((rows, width), jnp.bfloat16),
        in_specs=[vmem] * len(operands),
        out_specs=vmem,
        compiler_params=pltpu.CompilerParams(vmem_limit_bytes=40 * 2**20),
        cost_estimate=pl.CostEstimate(flops=flops, bytes_accessed=moved, transcendentals=rows * 2048),
    )(*operands)


def level_parts(count):
    level = jnp.arange(count, dtype=jnp.int32) % 4
    return jnp.where(level == 0, 2, jnp.where(level == 3, 1, 0))


def shards(tokens, gain_attn, weight_qkv, weight_out):
    lev_count, row_count, col_count, width = tokens.shape
    edge = EDGE * HALF * lev_count
    rows = row_count * HALF * lev_count
    halves = tokens.transpose(1, 2, 0, 3).reshape(row_count, 2, HALF, lev_count, width)
    own = halves.transpose(1, 0, 2, 3, 4).reshape(2, rows, width)
    east = shift(own[0], "lon", -1, True)
    west = shift(own[1], "lon", 1, True)
    south = shift(own[:, :edge], "lat", -1, False)
    north = shift(own[:, rows - edge :], "lat", 1, False)
    halos = jnp.stack([west, east])
    far_south = shift(halos[:, :edge], "lat", -1, False)
    far_north = shift(halos[:, rows - edge :], "lat", 1, False)

    gain = gain_attn.reshape(1, width)
    inner = rows - 2 * edge
    same = level_parts(inner)[:, None] == level_parts(2 * inner)[None, :]
    inner_bias = jnp.where(same, 0.0, FAR).astype(jnp.float32)
    same = level_parts(edge)[:, None] == level_parts(4 * edge)[None, :]
    here = jnp.arange(4 * edge) < 2 * edge
    place = lax.axis_index("lat")
    open_edges = jnp.stack([place > 0, place < lax.axis_size("lat") - 1])
    reach = same[None] & (here[None, None, :] | open_edges[:, None, None])
    edge_bias = jnp.where(reach, 0.0, FAR).astype(jnp.float32)

    middle = call(
        inner_kernel, 2 * inner, 1_400_000_000, own, west, east, inner_bias, gain, weight_qkv, weight_out
    )
    edges = call(
        edge_kernel,
        4 * edge,
        2_400_000_000,
        own,
        west,
        east,
        jnp.stack([north, south]),
        jnp.stack([far_north, far_south]),
        edge_bias,
        gain,
        weight_qkv,
        weight_out,
    )
    edges = edges.reshape(2, 2, edge, width)
    middle = middle.reshape(2, inner, width)
    mixed = jnp.concatenate([edges[0], middle, edges[1]], axis=1)
    mixed = mixed.reshape(2, row_count, HALF, lev_count, width).transpose(1, 0, 2, 3, 4)
    return mixed.reshape(row_count, col_count, lev_count, width).transpose(2, 0, 1, 3)


def solution(mesh):
    placed = (P(None, "lat", "lon", None), P(), P(), P())
    return jax.shard_map(
        shards, mesh=mesh, in_specs=placed, out_specs=P(None, "lat", "lon", None), check_vma=False
    )
```

```python
import jax
import jax.numpy as jnp
from jax import lax
from jax.experimental import pallas as pl
from jax.experimental.pallas import tpu as pltpu
from jax.sharding import PartitionSpec as P

HEADS = 8
HEAD_SIZE = 64
GROUP = 4
SPAN = GROUP * HEAD_SIZE
EPS = 1e-05
FAR = -1e30
HALF = 6
EDGE = 3
LEVELS = 4
RIM = EDGE * HALF * LEVELS


def shift(value, axis, by, wrap):
    count = lax.axis_size(axis)
    pairs = [(i, (i + by) % count) for i in range(count) if wrap or 0 <= i + by < count]
    return lax.ppermute(value, axis, pairs)


def layer_norm(values, gain):
    center = values - jnp.mean(values, axis=-1, keepdims=True)
    spread = jnp.mean(center * center, axis=-1, keepdims=True)
    return (center * lax.rsqrt(spread + EPS) * gain).astype(jnp.bfloat16)


def matmul(a, b):
    return jnp.dot(a, b, preferred_element_type=jnp.float32)


def rounded(values):
    return values.astype(jnp.bfloat16).astype(jnp.float32)


def level_bias(rows, keys):
    def part(axis):
        level = lax.broadcasted_iota(jnp.int32, (rows, keys), axis) % LEVELS
        return jnp.where(level == 0, 2, jnp.where(level == LEVELS - 1, 1, 0))

    return jnp.where(part(0) == part(1), 0.0, FAR).astype(jnp.float32)


def attend(query, keys, values, bias):
    rows = query.shape[0]
    owner = lax.broadcasted_iota(jnp.int32, (rows, SPAN), 1) // HEAD_SIZE
    tall = jnp.concatenate([bias] * GROUP, axis=0)

    def merge(tall_values):
        merged = jnp.broadcast_to(tall_values[:rows], (rows, SPAN))
        for h in range(1, GROUP):
            merged = jnp.where(owner == h, tall_values[h * rows : (h + 1) * rows], merged)
        return merged

    parts = []
    for start in range(0, query.shape[1], SPAN):
        piece = query[:, start : start + SPAN]
        spread = jnp.concatenate(
            [jnp.where(owner == h, piece, 0.0) for h in range(GROUP)], axis=0
        ).astype(jnp.bfloat16)
        scores = lax.dot_general(
            spread,
            keys[:, start : start + SPAN],
            (((1,), (1,)), ((), ())),
            preferred_element_type=jnp.float32,
        )
        scores = scores + tall
        top = jnp.max(scores, axis=-1, keepdims=True)
        expo = jnp.exp(scores - top)
        total = jnp.sum(expo, axis=-1, keepdims=True)
        out = matmul(expo.astype(jnp.bfloat16), values[:, start : start + SPAN])
        parts.append((merge(out), merge(top), merge(total)))
    return tuple(jnp.concatenate(p, axis=1) for p in zip(*parts))


def add_keys(state, more):
    out, top, total = state
    out_2, top_2, total_2 = more
    peak = jnp.maximum(top, top_2)
    old, new = jnp.exp(top - peak), jnp.exp(top_2 - peak)
    return out * old + out_2 * new, peak, total * old + total_2 * new


def load(ref, at):
    return tuple(ref[i, at] for i in range(3))


def store(ref, at, state):
    for i in range(3):
        ref[i, at] = state[i]


def project(tokens, state, weight_ref):
    out, _, total = state
    branch = matmul((out / total).astype(jnp.bfloat16), weight_ref[...])
    return (tokens + rounded(branch)).astype(jnp.bfloat16)


def own_kernel(closed_ref, west_ref, east_ref, north_ref, south_ref, gain_ref, qkv_ref, query_ref, state_ref):
    width = west_ref.shape[-1]
    rows = west_ref.shape[0]
    gain = gain_ref[...]
    mine = jnp.concatenate([r[...].astype(jnp.float32) for r in (west_ref, east_ref)], axis=0)
    theirs = jnp.concatenate([r[s].astype(jnp.float32) for r in (north_ref, south_ref) for s in range(2)], axis=0)
    mine = layer_norm(mine, gain)
    theirs = layer_norm(theirs, gain)
    query = rounded(matmul(mine, qkv_ref[:, :width])) * HEAD_SIZE**-0.5
    query_ref[...] = query
    mine = matmul(mine, qkv_ref[:, width:])
    theirs = matmul(theirs, qkv_ref[:, width:])
    inner = level_bias(rows - 2 * RIM, rows - 2 * RIM)
    rim = level_bias(RIM, 2 * RIM)
    distant = lax.broadcasted_iota(jnp.int32, (RIM, 2 * RIM), 1) >= RIM
    for side in range(2):
        base = side * rows
        at = slice(base + RIM, base + rows - RIM)
        kv = mine[at].astype(jnp.bfloat16)
        store(state_ref, at, attend(query[at], kv[:, :width], kv[:, width:], inner))
        for edge in range(2):
            begin = base + edge * (rows - RIM)
            at = slice(begin, begin + RIM)
            beyond = (edge * 2 + side) * RIM
            kv = jnp.concatenate([mine[at], theirs[beyond : beyond + RIM]], axis=0).astype(jnp.bfloat16)
            bias = rim + jnp.where(distant, closed_ref[edge], 0.0)
            store(state_ref, at, attend(query[at], kv[:, :width], kv[:, width:], bias))


def halo_kernel(
    query_ref, state_ref, own_w_ref, own_e_ref, west_ref, east_ref, gain_ref, qkv_ref, out_w_ref, out_ref, rim_ref
):
    width = west_ref.shape[-1]
    rows = west_ref.shape[0]
    halos = jnp.concatenate([r[...].astype(jnp.float32) for r in (west_ref, east_ref)], axis=0)
    halos = matmul(layer_norm(halos, gain_ref[...]), qkv_ref[:, width:])
    inner = level_bias(rows - 2 * RIM, rows - 2 * RIM)
    rim = level_bias(RIM, RIM)
    done, tokens = [], []
    for side in range(2):
        base = side * rows
        for edge in range(2):
            begin = base + edge * (rows - RIM)
            at = slice(begin, begin + RIM)
            kv = halos[at].astype(jnp.bfloat16)
            more = attend(query_ref[at], kv[:, :width], kv[:, width:], rim)
            place = (edge * 2 + side) * RIM
            store(rim_ref, slice(place, place + RIM), add_keys(load(state_ref, at), more))
        at = slice(base + RIM, base + rows - RIM)
        kv = halos[at].astype(jnp.bfloat16)
        more = attend(query_ref[at], kv[:, :width], kv[:, width:], inner)
        done.append(add_keys(load(state_ref, at), more))
        tokens.append((own_w_ref, own_e_ref)[side][...].astype(jnp.float32)[RIM : rows - RIM])
    done = tuple(jnp.concatenate(p, axis=0) for p in zip(*done))
    out_ref[...] = project(jnp.concatenate(tokens, axis=0), done, out_w_ref)


def corner_kernel(
    closed_ref,
    query_ref,
    rim_ref,
    own_w_ref,
    own_e_ref,
    north_ref,
    south_ref,
    middle_ref,
    gain_ref,
    qkv_ref,
    out_w_ref,
    out_ref,
):
    width = own_w_ref.shape[-1]
    rows = own_w_ref.shape[0]
    corners = jnp.concatenate([r[s].astype(jnp.float32) for r in (north_ref, south_ref) for s in range(2)], axis=0)
    corners = matmul(layer_norm(corners, gain_ref[...]), qkv_ref[:, width:])
    rim = level_bias(RIM, RIM)
    own = [r[...].astype(jnp.float32) for r in (own_w_ref, own_e_ref)]
    done, tokens = [], []
    for edge in range(2):
        for side in range(2):
            begin = edge * (rows - RIM)
            at = slice(begin, begin + RIM)
            place = (edge * 2 + side) * RIM
            kv = corners[place : place + RIM].astype(jnp.bfloat16)
            query = query_ref[slice(side * rows + begin, side * rows + begin + RIM)]
            more = attend(query, kv[:, :width], kv[:, width:], rim + closed_ref[edge])
            done.append(add_keys(load(rim_ref, slice(place, place + RIM)), more))
            tokens.append(own[side][at])
    done = tuple(jnp.concatenate(p, axis=0) for p in zip(*done))
    mixed = project(jnp.concatenate(tokens, axis=0), done, out_w_ref).astype(jnp.float32)
    middle = middle_ref[...].astype(jnp.float32)
    count = rows - 2 * RIM
    for side in range(2):
        out_ref[side] = jnp.concatenate(
            [
                mixed[side * RIM : (side + 1) * RIM],
                middle[side * count : (side + 1) * count],
                mixed[(2 + side) * RIM : (3 + side) * RIM],
            ],
            axis=0,
        ).astype(jnp.bfloat16)


def call(kernel, results, flops, *operands):
    moved = sum(x.size * x.dtype.itemsize for x in (*operands, *results))
    specs = [pl.BlockSpec(memory_space=pltpu.SMEM if x.ndim == 1 else pltpu.VMEM) for x in operands]
    return pl.pallas_call(
        kernel,
        out_shape=results,
        in_specs=specs,
        out_specs=[pl.BlockSpec(memory_space=pltpu.VMEM)] * len(results),
        compiler_params=pltpu.CompilerParams(vmem_limit_bytes=40 * 2**20),
        cost_estimate=pl.CostEstimate(flops=flops, bytes_accessed=moved, transcendentals=0),
    )(*operands)


def shards(tokens, gain_attn, weight_qkv, weight_out):
    lev_count, row_count, col_count, width = tokens.shape
    rows = row_count * HALF * lev_count
    by_place = tokens.transpose(1, 2, 0, 3)
    own_w = by_place[:, :HALF].reshape(rows, width)
    own_e = by_place[:, HALF:].reshape(rows, width)
    east = shift(own_w, "lon", -1, True)
    west = shift(own_e, "lon", 1, True)

    def both(a, b, at):
        return jnp.stack([a[at], b[at]])

    top, bottom = slice(0, RIM), slice(rows - RIM, rows)
    south = shift(both(own_w, own_e, top), "lat", -1, False)
    north = shift(both(own_w, own_e, bottom), "lat", 1, False)
    far_south = shift(both(west, east, top), "lat", -1, False)
    far_north = shift(both(west, east, bottom), "lat", 1, False)

    gain = gain_attn.reshape(1, width)
    place = lax.axis_index("lat")
    closed = jnp.stack([place == 0, place == lax.axis_size("lat") - 1])
    closed = jnp.where(closed, FAR, 0.0).astype(jnp.float32)

    def shape(*dims, dtype=jnp.float32):
        return jax.ShapeDtypeStruct(dims, dtype)

    query, state = call(
        own_kernel,
        [shape(2 * rows, width), shape(3, 2 * rows, width)],
        2_400_000_000,
        closed,
        own_w,
        own_e,
        north,
        south,
        gain,
        weight_qkv,
    )
    middle, rim = call(
        halo_kernel,
        [shape(2 * (rows - 2 * RIM), width, dtype=jnp.bfloat16), shape(3, 4 * RIM, width)],
        1_500_000_000,
        query,
        state,
        own_w,
        own_e,
        west,
        east,
        gain,
        weight_qkv,
        weight_out,
    )
    (mixed,) = call(
        corner_kernel,
        [shape(2, rows, width, dtype=jnp.bfloat16)],
        1_000_000_000,
        closed,
        query,
        rim,
        own_w,
        own_e,
        far_north,
        far_south,
        middle,
        gain,
        weight_qkv,
        weight_out,
    )
    mixed = mixed.reshape(2, row_count, HALF, lev_count, width).transpose(1, 0, 2, 3, 4)
    return mixed.reshape(row_count, col_count, lev_count, width).transpose(2, 0, 1, 3)


def solution(mesh):
    placed = (P(None, "lat", "lon", None), P(), P(), P())
    return jax.shard_map(
        shards, mesh=mesh, in_specs=placed, out_specs=P(None, "lat", "lon", None), check_vma=False
    )
```

```python
import jax
import jax.numpy as jnp
from jax import lax
from jax.experimental import pallas as pl
from jax.experimental.pallas import tpu as pltpu
from jax.sharding import PartitionSpec as P

HEADS = 8
HEAD_SIZE = 64
GROUP = 4
SPAN = GROUP * HEAD_SIZE
EPS = 1e-05
FAR = -1e30
HALF = 6
EDGE = 3
LEVELS = 4
RIM = EDGE * HALF * LEVELS


def shift(value, axis, by, wrap):
    count = lax.axis_size(axis)
    pairs = [(i, (i + by) % count) for i in range(count) if wrap or 0 <= i + by < count]
    return lax.ppermute(value, axis, pairs)


def layer_norm(values, gain):
    center = values - jnp.mean(values, axis=-1, keepdims=True)
    spread = jnp.mean(center * center, axis=-1, keepdims=True)
    return (center * lax.rsqrt(spread + EPS) * gain).astype(jnp.bfloat16)


def matmul(a, b):
    return jnp.dot(a, b, preferred_element_type=jnp.float32)


def rounded(values):
    return values.astype(jnp.bfloat16).astype(jnp.float32)


def level_bias(rows, keys):
    def part(axis):
        level = lax.broadcasted_iota(jnp.int32, (rows, keys), axis) % LEVELS
        return jnp.where(level == 0, 2, jnp.where(level == LEVELS - 1, 1, 0))

    return jnp.where(part(0) == part(1), 0.0, FAR).astype(jnp.float32)


def attend(query, keys, values, bias):
    rows = query.shape[0]
    owner = lax.broadcasted_iota(jnp.int32, (rows, SPAN), 1) // HEAD_SIZE
    tall = jnp.concatenate([bias] * GROUP, axis=0)

    def merge(tall_values):
        merged = jnp.broadcast_to(tall_values[:rows], (rows, SPAN))
        for h in range(1, GROUP):
            merged = jnp.where(owner == h, tall_values[h * rows : (h + 1) * rows], merged)
        return merged

    parts = []
    for start in range(0, query.shape[1], SPAN):
        piece = query[:, start : start + SPAN]
        spread = jnp.concatenate(
            [jnp.where(owner == h, piece, 0.0) for h in range(GROUP)], axis=0
        ).astype(jnp.bfloat16)
        scores = lax.dot_general(
            spread,
            keys[:, start : start + SPAN],
            (((1,), (1,)), ((), ())),
            preferred_element_type=jnp.float32,
        )
        scores = scores + tall
        top = jnp.max(scores, axis=-1, keepdims=True)
        expo = jnp.exp(scores - top)
        total = jnp.sum(expo, axis=-1, keepdims=True)
        out = matmul(expo.astype(jnp.bfloat16), values[:, start : start + SPAN])
        parts.append((merge(out), merge(top), merge(total)))
    return tuple(jnp.concatenate(p, axis=1) for p in zip(*parts))


def add_keys(state, more):
    out, top, total = state
    out_2, top_2, total_2 = more
    peak = jnp.maximum(top, top_2)
    old, new = jnp.exp(top - peak), jnp.exp(top_2 - peak)
    return out * old + out_2 * new, peak, total * old + total_2 * new


def load(ref, at):
    return tuple(ref[i, at] for i in range(3))


def store(ref, at, state):
    for i in range(3):
        ref[i, at] = state[i]


def project(tokens, state, weight_ref):
    out, _, total = state
    branch = matmul((out / total).astype(jnp.bfloat16), weight_ref[...])
    return (tokens + rounded(branch)).astype(jnp.bfloat16)


def own_kernel(west_ref, east_ref, gain_ref, qkv_ref, query_ref, inner_ref, rim_ref):
    width = west_ref.shape[-1]
    rows = west_ref.shape[0]
    mine = jnp.concatenate([r[...].astype(jnp.float32) for r in (west_ref, east_ref)], axis=0)
    mine = layer_norm(mine, gain_ref[...])
    query = rounded(matmul(mine, qkv_ref[:, :width])) * HEAD_SIZE**-0.5
    query_ref[...] = query
    mine = matmul(mine, qkv_ref[:, width:])
    add_halves(query, mine, inner_ref, rim_ref)


def add_halves(query, kv_all, inner_ref, rim_ref, inner_before=None, rim_before=None):
    rows = kv_all.shape[0] // 2
    width = query.shape[-1]
    count = rows - 2 * RIM
    inner = level_bias(count, count)
    rim = level_bias(RIM, RIM)
    done = []
    for side in range(2):
        base = side * rows
        for edge in range(2):
            begin = base + edge * (rows - RIM)
            at = slice(begin, begin + RIM)
            kv = kv_all[at].astype(jnp.bfloat16)
            more = attend(query[at], kv[:, :width], kv[:, width:], rim)
            place = slice((edge * 2 + side) * RIM, (edge * 2 + side + 1) * RIM)
            store(rim_ref, place, more if rim_before is None else add_keys(load(rim_before, place), more))
        at = slice(base + RIM, base + rows - RIM)
        kv = kv_all[at].astype(jnp.bfloat16)
        more = attend(query[at], kv[:, :width], kv[:, width:], inner)
        place = slice(side * count, (side + 1) * count)
        if inner_before is None:
            store(inner_ref, place, more)
        else:
            done.append(add_keys(load(inner_before, place), more))
    return done


def halo_kernel(
    query_ref, inner_ref, rim_ref, own_w_ref, own_e_ref, west_ref, east_ref, gain_ref, qkv_ref, out_w_ref, out_ref, rim_out_ref
):
    width = west_ref.shape[-1]
    rows = west_ref.shape[0]
    halos = jnp.concatenate([r[...].astype(jnp.float32) for r in (west_ref, east_ref)], axis=0)
    halos = matmul(layer_norm(halos, gain_ref[...]), qkv_ref[:, width:])
    done = add_halves(query_ref[...], halos, None, rim_out_ref, inner_ref, rim_ref)
    done = tuple(jnp.concatenate(p, axis=0) for p in zip(*done))
    tokens = [r[...].astype(jnp.float32)[RIM : rows - RIM] for r in (own_w_ref, own_e_ref)]
    out_ref[...] = project(jnp.concatenate(tokens, axis=0), done, out_w_ref)


def add_rims(closed_ref, query_ref, rim_ref, north_ref, south_ref, gain_ref, qkv_ref):
    width = query_ref.shape[-1]
    rows = query_ref.shape[0] // 2
    beyond = jnp.concatenate([r[s].astype(jnp.float32) for r in (north_ref, south_ref) for s in range(2)], axis=0)
    beyond = matmul(layer_norm(beyond, gain_ref[...]), qkv_ref[:, width:])
    rim = level_bias(RIM, RIM)
    done = []
    for edge in range(2):
        for side in range(2):
            begin = side * rows + edge * (rows - RIM)
            place = slice((edge * 2 + side) * RIM, (edge * 2 + side + 1) * RIM)
            kv = beyond[place].astype(jnp.bfloat16)
            query = query_ref[begin : begin + RIM]
            more = attend(query, kv[:, :width], kv[:, width:], rim + closed_ref[edge])
            done.append(add_keys(load(rim_ref, place), more))
    return done


def latitude_kernel(closed_ref, query_ref, rim_ref, north_ref, south_ref, gain_ref, qkv_ref, rim_out_ref):
    done = add_rims(closed_ref, query_ref, rim_ref, north_ref, south_ref, gain_ref, qkv_ref)
    for place, state in enumerate(done):
        store(rim_out_ref, slice(place * RIM, (place + 1) * RIM), state)


def corner_kernel(
    closed_ref,
    query_ref,
    rim_ref,
    north_ref,
    south_ref,
    gain_ref,
    qkv_ref,
    own_w_ref,
    own_e_ref,
    middle_ref,
    out_w_ref,
    out_ref,
):
    rows = own_w_ref.shape[0]
    done = add_rims(closed_ref, query_ref, rim_ref, north_ref, south_ref, gain_ref, qkv_ref)
    done = tuple(jnp.concatenate(p, axis=0) for p in zip(*done))
    own = [r[...].astype(jnp.float32) for r in (own_w_ref, own_e_ref)]
    tokens = [half[at] for at in (slice(0, RIM), slice(rows - RIM, rows)) for half in own]
    mixed = project(jnp.concatenate(tokens, axis=0), done, out_w_ref).astype(jnp.float32)
    middle = middle_ref[...].astype(jnp.float32)
    count = rows - 2 * RIM
    for side in range(2):
        out_ref[side] = jnp.concatenate(
            [
                mixed[side * RIM : (side + 1) * RIM],
                middle[side * count : (side + 1) * count],
                mixed[(2 + side) * RIM : (3 + side) * RIM],
            ],
            axis=0,
        ).astype(jnp.bfloat16)


def call(kernel, results, flops, *operands):
    moved = sum(x.size * x.dtype.itemsize for x in (*operands, *results))
    specs = [pl.BlockSpec(memory_space=pltpu.SMEM if x.ndim == 1 else pltpu.VMEM) for x in operands]
    return pl.pallas_call(
        kernel,
        out_shape=results,
        in_specs=specs,
        out_specs=[pl.BlockSpec(memory_space=pltpu.VMEM)] * len(results),
        compiler_params=pltpu.CompilerParams(vmem_limit_bytes=40 * 2**20),
        cost_estimate=pl.CostEstimate(flops=flops, bytes_accessed=moved, transcendentals=0),
    )(*operands)


def shards(tokens, gain_attn, weight_qkv, weight_out):
    lev_count, row_count, col_count, width = tokens.shape
    rows = row_count * HALF * lev_count
    by_place = tokens.transpose(1, 2, 0, 3)
    own_w = by_place[:, :HALF].reshape(rows, width)
    own_e = by_place[:, HALF:].reshape(rows, width)
    east = shift(own_w, "lon", -1, True)
    west = shift(own_e, "lon", 1, True)

    def both(a, b, at):
        return jnp.stack([a[at], b[at]])

    top, bottom = slice(0, RIM), slice(rows - RIM, rows)
    gain = gain_attn.reshape(1, width)
    place = lax.axis_index("lat")
    closed = jnp.stack([place == 0, place == lax.axis_size("lat") - 1])
    closed = jnp.where(closed, FAR, 0.0).astype(jnp.float32)

    def shape(*dims, dtype=jnp.float32):
        return jax.ShapeDtypeStruct(dims, dtype)

    inner_shape = shape(3, 2 * (rows - 2 * RIM), width)
    rim_shape = shape(3, 4 * RIM, width)
    query, inner, rim = call(
        own_kernel,
        [shape(2 * rows, width), inner_shape, rim_shape],
        2_000_000_000,
        own_w,
        own_e,
        gain,
        weight_qkv,
    )
    lat_w, lat_e, query, rim = lax.optimization_barrier((own_w, own_e, query, rim))
    south = shift(both(lat_w, lat_e, top), "lat", -1, False)
    north = shift(both(lat_w, lat_e, bottom), "lat", 1, False)
    (rim,) = call(latitude_kernel, [rim_shape], 800_000_000, closed, query, rim, north, south, gain, weight_qkv)
    west, east, query, rim = lax.optimization_barrier((west, east, query, rim))
    far_south = shift(both(west, east, top), "lat", -1, False)
    far_north = shift(both(west, east, bottom), "lat", 1, False)
    middle, rim = call(
        halo_kernel,
        [shape(2 * (rows - 2 * RIM), width, dtype=jnp.bfloat16), rim_shape],
        1_500_000_000,
        query,
        inner,
        rim,
        own_w,
        own_e,
        west,
        east,
        gain,
        weight_qkv,
        weight_out,
    )
    (mixed,) = call(
        corner_kernel,
        [shape(2, rows, width, dtype=jnp.bfloat16)],
        1_000_000_000,
        closed,
        query,
        rim,
        far_north,
        far_south,
        gain,
        weight_qkv,
        own_w,
        own_e,
        middle,
        weight_out,
    )
    mixed = mixed.reshape(2, row_count, HALF, lev_count, width).transpose(1, 0, 2, 3, 4)
    return mixed.reshape(row_count, col_count, lev_count, width).transpose(2, 0, 1, 3)


def solution(mesh):
    placed = (P(None, "lat", "lon", None), P(), P(), P())
    return jax.shard_map(
        shards, mesh=mesh, in_specs=placed, out_specs=P(None, "lat", "lon", None), check_vma=False
    )
```

```python
import jax
import jax.numpy as jnp
from jax import lax
from jax.experimental import pallas as pl
from jax.experimental.pallas import tpu as pltpu
from jax.sharding import PartitionSpec as P

HEADS = 8
HEAD_SIZE = 64
GROUP = 4
SPAN = GROUP * HEAD_SIZE
EPS = 1e-05
FAR = -1e30
HALF = 6
EDGE = 3
LEVELS = 4
RIM = EDGE * HALF * LEVELS


def shift(value, axis, by, wrap):
    count = lax.axis_size(axis)
    pairs = [(i, (i + by) % count) for i in range(count) if wrap or 0 <= i + by < count]
    return lax.ppermute(value, axis, pairs)


def layer_norm(values, gain):
    center = values - jnp.mean(values, axis=-1, keepdims=True)
    spread = jnp.mean(center * center, axis=-1, keepdims=True)
    return (center * lax.rsqrt(spread + EPS) * gain).astype(jnp.bfloat16)


def matmul(a, b):
    return jnp.dot(a, b, preferred_element_type=jnp.float32)


def rounded(values):
    return values.astype(jnp.bfloat16).astype(jnp.float32)


def level_bias(rows, keys):
    def part(axis):
        level = lax.broadcasted_iota(jnp.int32, (rows, keys), axis) % LEVELS
        return jnp.where(level == 0, 2, jnp.where(level == LEVELS - 1, 1, 0))

    return jnp.where(part(0) == part(1), 0.0, FAR).astype(jnp.float32)


def attend(query, keys, values, bias):
    rows = query.shape[0]
    owner = lax.broadcasted_iota(jnp.int32, (rows, SPAN), 1) // HEAD_SIZE
    tall = jnp.concatenate([bias] * GROUP, axis=0)

    def merge(tall_values):
        merged = jnp.broadcast_to(tall_values[:rows], (rows, SPAN))
        for h in range(1, GROUP):
            merged = jnp.where(owner == h, tall_values[h * rows : (h + 1) * rows], merged)
        return merged

    parts = []
    for start in range(0, query.shape[1], SPAN):
        piece = query[:, start : start + SPAN]
        spread = jnp.concatenate(
            [jnp.where(owner == h, piece, 0.0) for h in range(GROUP)], axis=0
        ).astype(jnp.bfloat16)
        scores = lax.dot_general(
            spread,
            keys[:, start : start + SPAN],
            (((1,), (1,)), ((), ())),
            preferred_element_type=jnp.float32,
        )
        scores = scores + tall
        top = jnp.max(scores, axis=-1, keepdims=True)
        expo = jnp.exp(scores - top)
        total = jnp.sum(expo, axis=-1, keepdims=True)
        out = matmul(expo.astype(jnp.bfloat16), values[:, start : start + SPAN])
        parts.append((merge(out), merge(top), merge(total)))
    return tuple(jnp.concatenate(p, axis=1) for p in zip(*parts))


def add_keys(state, more):
    out, top, total = state
    out_2, top_2, total_2 = more
    peak = jnp.maximum(top, top_2)
    old, new = jnp.exp(top - peak), jnp.exp(top_2 - peak)
    return out * old + out_2 * new, peak, total * old + total_2 * new


def load(ref, at):
    return tuple(ref[i, at] for i in range(3))


def store(ref, at, state):
    for i in range(3):
        ref[i, at] = state[i]


def project(tokens, state, weight_ref):
    out, _, total = state
    branch = matmul((out / total).astype(jnp.bfloat16), weight_ref[...])
    return (tokens + rounded(branch)).astype(jnp.bfloat16)


def own_kernel(west_ref, east_ref, gain_ref, qkv_ref, query_ref, inner_ref, rim_ref, ready_ref):
    ready_ref[...] = jnp.zeros_like(ready_ref)
    width = west_ref.shape[-1]
    rows = west_ref.shape[0]
    mine = jnp.concatenate([r[...].astype(jnp.float32) for r in (west_ref, east_ref)], axis=0)
    mine = layer_norm(mine, gain_ref[...])
    query = rounded(matmul(mine, qkv_ref[:, :width])) * HEAD_SIZE**-0.5
    query_ref[...] = query
    mine = matmul(mine, qkv_ref[:, width:])
    add_halves(query, mine, inner_ref, rim_ref)


def add_halves(query, kv_all, inner_ref, rim_ref, inner_before=None, rim_before=None):
    rows = kv_all.shape[0] // 2
    width = query.shape[-1]
    count = rows - 2 * RIM
    inner = level_bias(count, count)
    rim = level_bias(RIM, RIM)
    done = []
    for side in range(2):
        base = side * rows
        for edge in range(2):
            begin = base + edge * (rows - RIM)
            at = slice(begin, begin + RIM)
            kv = kv_all[at].astype(jnp.bfloat16)
            more = attend(query[at], kv[:, :width], kv[:, width:], rim)
            place = slice((edge * 2 + side) * RIM, (edge * 2 + side + 1) * RIM)
            store(rim_ref, place, more if rim_before is None else add_keys(load(rim_before, place), more))
        at = slice(base + RIM, base + rows - RIM)
        kv = kv_all[at].astype(jnp.bfloat16)
        more = attend(query[at], kv[:, :width], kv[:, width:], inner)
        place = slice(side * count, (side + 1) * count)
        if inner_before is None:
            store(inner_ref, place, more)
        else:
            done.append(add_keys(load(inner_before, place), more))
    return done


def pack_kernel(ready_ref, *refs):
    *parts, south_ref, north_ref = refs
    rows = parts[0].shape[0]
    for i, part in enumerate(parts):
        values = part[...].astype(jnp.float32)
        south_ref[i] = values[:RIM].astype(jnp.bfloat16)
        north_ref[i] = values[rows - RIM :].astype(jnp.bfloat16)


def halo_kernel(
    query_ref, inner_ref, rim_ref, own_w_ref, own_e_ref, west_ref, east_ref, gain_ref, qkv_ref, out_w_ref, out_ref, rim_out_ref
):
    width = west_ref.shape[-1]
    rows = west_ref.shape[0]
    halos = jnp.concatenate([r[...].astype(jnp.float32) for r in (west_ref, east_ref)], axis=0)
    halos = matmul(layer_norm(halos, gain_ref[...]), qkv_ref[:, width:])
    done = add_halves(query_ref[...], halos, None, rim_out_ref, inner_ref, rim_ref)
    done = tuple(jnp.concatenate(p, axis=0) for p in zip(*done))
    tokens = [r[...].astype(jnp.float32)[RIM : rows - RIM] for r in (own_w_ref, own_e_ref)]
    out_ref[...] = project(jnp.concatenate(tokens, axis=0), done, out_w_ref)


def add_rims(closed_ref, query_ref, rim_ref, north_ref, south_ref, gain_ref, qkv_ref):
    width = query_ref.shape[-1]
    rows = query_ref.shape[0] // 2
    beyond = jnp.concatenate([r[p].astype(jnp.float32) for r in (north_ref, south_ref) for p in range(4)], axis=0)
    beyond = matmul(layer_norm(beyond, gain_ref[...]), qkv_ref[:, width:])
    rim = level_bias(RIM, 2 * RIM)
    done = []
    for edge in range(2):
        for side in range(2):
            begin = side * rows + edge * (rows - RIM)
            place = slice((edge * 2 + side) * RIM, (edge * 2 + side + 1) * RIM)
            first, second = ((edge * 4 + part) * RIM for part in (side, side + 2))
            kv = jnp.concatenate([beyond[first : first + RIM], beyond[second : second + RIM]], axis=0)
            kv = kv.astype(jnp.bfloat16)
            query = query_ref[begin : begin + RIM]
            more = attend(query, kv[:, :width], kv[:, width:], rim + closed_ref[edge])
            done.append(add_keys(load(rim_ref, place), more))
    return done


def corner_kernel(
    closed_ref,
    query_ref,
    rim_ref,
    north_ref,
    south_ref,
    gain_ref,
    qkv_ref,
    own_w_ref,
    own_e_ref,
    middle_ref,
    out_w_ref,
    out_ref,
):
    rows = own_w_ref.shape[0]
    done = add_rims(closed_ref, query_ref, rim_ref, north_ref, south_ref, gain_ref, qkv_ref)
    done = tuple(jnp.concatenate(p, axis=0) for p in zip(*done))
    own = [r[...].astype(jnp.float32) for r in (own_w_ref, own_e_ref)]
    tokens = [half[at] for at in (slice(0, RIM), slice(rows - RIM, rows)) for half in own]
    mixed = project(jnp.concatenate(tokens, axis=0), done, out_w_ref).astype(jnp.float32)
    middle = middle_ref[...].astype(jnp.float32)
    count = rows - 2 * RIM
    for side in range(2):
        out_ref[side] = jnp.concatenate(
            [
                mixed[side * RIM : (side + 1) * RIM],
                middle[side * count : (side + 1) * count],
                mixed[(2 + side) * RIM : (3 + side) * RIM],
            ],
            axis=0,
        ).astype(jnp.bfloat16)


def call(kernel, results, flops, *operands):
    moved = sum(x.size * x.dtype.itemsize for x in (*operands, *results))
    specs = [pl.BlockSpec(memory_space=pltpu.SMEM if x.ndim == 1 else pltpu.VMEM) for x in operands]
    return pl.pallas_call(
        kernel,
        out_shape=results,
        in_specs=specs,
        out_specs=[pl.BlockSpec(memory_space=pltpu.VMEM)] * len(results),
        compiler_params=pltpu.CompilerParams(vmem_limit_bytes=40 * 2**20),
        cost_estimate=pl.CostEstimate(flops=flops, bytes_accessed=moved, transcendentals=0),
    )(*operands)


def shards(tokens, gain_attn, weight_qkv, weight_out):
    lev_count, row_count, col_count, width = tokens.shape
    rows = row_count * HALF * lev_count
    by_place = tokens.transpose(1, 2, 0, 3)
    own_w = by_place[:, :HALF].reshape(rows, width)
    own_e = by_place[:, HALF:].reshape(rows, width)
    east = shift(own_w, "lon", -1, True)
    west = shift(own_e, "lon", 1, True)
    gain = gain_attn.reshape(1, width)
    place = lax.axis_index("lat")
    closed = jnp.stack([place == 0, place == lax.axis_size("lat") - 1])
    closed = jnp.where(closed, FAR, 0.0).astype(jnp.float32)

    def shape(*dims, dtype=jnp.float32):
        return jax.ShapeDtypeStruct(dims, dtype)

    inner_shape = shape(3, 2 * (rows - 2 * RIM), width)
    rim_shape = shape(3, 4 * RIM, width)
    query, inner, rim, ready = call(
        own_kernel,
        [shape(2 * rows, width), inner_shape, rim_shape, shape(8, 128)],
        2_000_000_000,
        own_w,
        own_e,
        gain,
        weight_qkv,
    )
    packed = shape(4, RIM, width, dtype=jnp.bfloat16)
    to_south, to_north = call(pack_kernel, [packed, packed], 1_000_000, ready, own_w, own_e, west, east)
    far_south = shift(to_south, "lat", -1, False)
    far_north = shift(to_north, "lat", 1, False)
    middle, rim = call(
        halo_kernel,
        [shape(2 * (rows - 2 * RIM), width, dtype=jnp.bfloat16), rim_shape],
        1_500_000_000,
        query,
        inner,
        rim,
        own_w,
        own_e,
        west,
        east,
        gain,
        weight_qkv,
        weight_out,
    )
    (mixed,) = call(
        corner_kernel,
        [shape(2, rows, width, dtype=jnp.bfloat16)],
        1_000_000_000,
        closed,
        query,
        rim,
        far_north,
        far_south,
        gain,
        weight_qkv,
        own_w,
        own_e,
        middle,
        weight_out,
    )
    mixed = mixed.reshape(2, row_count, HALF, lev_count, width).transpose(1, 0, 2, 3, 4)
    return mixed.reshape(row_count, col_count, lev_count, width).transpose(2, 0, 1, 3)


def solution(mesh):
    placed = (P(None, "lat", "lon", None), P(), P(), P())
    return jax.shard_map(
        shards, mesh=mesh, in_specs=placed, out_specs=P(None, "lat", "lon", None), check_vma=False
    )
```

```python
import jax
import jax.numpy as jnp
from jax import lax
from jax.experimental import pallas as pl
from jax.experimental.pallas import tpu as pltpu
from jax.sharding import PartitionSpec as P

HEADS = 8
HEAD_SIZE = 64
GROUP = 4
SPAN = GROUP * HEAD_SIZE
EPS = 1e-05
FAR = -1e30
HALF = 6
EDGE = 3
LEVELS = 4
RIM = EDGE * HALF * LEVELS


def shift(value, axis, by, wrap):
    count = lax.axis_size(axis)
    pairs = [(i, (i + by) % count) for i in range(count) if wrap or 0 <= i + by < count]
    return lax.ppermute(value, axis, pairs)


def layer_norm(values, gain):
    center = values - jnp.mean(values, axis=-1, keepdims=True)
    spread = jnp.mean(center * center, axis=-1, keepdims=True)
    return (center * lax.rsqrt(spread + EPS) * gain).astype(jnp.bfloat16)


def matmul(a, b):
    return jnp.dot(a, b, preferred_element_type=jnp.float32)


def rounded(values):
    return values.astype(jnp.bfloat16).astype(jnp.float32)


def level_bias(rows, keys):
    def part(axis):
        level = lax.broadcasted_iota(jnp.int32, (rows, keys), axis) % LEVELS
        return jnp.where(level == 0, 2, jnp.where(level == LEVELS - 1, 1, 0))

    return jnp.where(part(0) == part(1), 0.0, FAR).astype(jnp.float32)


def attend(query, keys, values, bias):
    rows = query.shape[0]
    owner = lax.broadcasted_iota(jnp.int32, (rows, SPAN), 1) // HEAD_SIZE
    tall = jnp.concatenate([bias] * GROUP, axis=0)

    def merge(tall_values):
        merged = jnp.broadcast_to(tall_values[:rows], (rows, SPAN))
        for h in range(1, GROUP):
            merged = jnp.where(owner == h, tall_values[h * rows : (h + 1) * rows], merged)
        return merged

    parts = []
    for start in range(0, query.shape[1], SPAN):
        piece = query[:, start : start + SPAN]
        spread = jnp.concatenate(
            [jnp.where(owner == h, piece, 0.0) for h in range(GROUP)], axis=0
        ).astype(jnp.bfloat16)
        scores = lax.dot_general(
            spread,
            keys[:, start : start + SPAN],
            (((1,), (1,)), ((), ())),
            preferred_element_type=jnp.float32,
        )
        scores = scores + tall
        top = jnp.max(scores, axis=-1, keepdims=True)
        expo = jnp.exp(scores - top)
        total = jnp.sum(expo, axis=-1, keepdims=True)
        out = matmul(expo.astype(jnp.bfloat16), values[:, start : start + SPAN])
        parts.append((merge(out), merge(top), merge(total)))
    return tuple(jnp.concatenate(p, axis=1) for p in zip(*parts))


def add_keys(state, more):
    out, top, total = state
    out_2, top_2, total_2 = more
    peak = jnp.maximum(top, top_2)
    old, new = jnp.exp(top - peak), jnp.exp(top_2 - peak)
    return out * old + out_2 * new, peak, total * old + total_2 * new


def load(ref, at):
    return tuple(ref[i, at] for i in range(3))


def store(ref, at, state):
    for i in range(3):
        ref[i, at] = state[i]


def project(tokens, state, weight_ref):
    out, _, total = state
    branch = matmul((out / total).astype(jnp.bfloat16), weight_ref[...])
    return (tokens + rounded(branch)).astype(jnp.bfloat16)


def own_kernel(west_ref, east_ref, gain_ref, qkv_ref, query_ref, inner_ref, rim_ref, ready_ref):
    ready_ref[...] = jnp.zeros_like(ready_ref)
    width = west_ref.shape[-1]
    rows = west_ref.shape[0]
    mine = jnp.concatenate([r[...].astype(jnp.float32) for r in (west_ref, east_ref)], axis=0)
    mine = layer_norm(mine, gain_ref[...])
    query = rounded(matmul(mine, qkv_ref[:, :width])) * HEAD_SIZE**-0.5
    query_ref[...] = query
    mine = matmul(mine, qkv_ref[:, width:])
    add_halves(query, mine, inner_ref, rim_ref)


def add_halves(query, kv_all, inner_ref, rim_ref, inner_before=None, rim_before=None):
    rows = kv_all.shape[0] // 2
    width = query.shape[-1]
    count = rows - 2 * RIM
    inner = level_bias(count, count)
    rim = level_bias(RIM, RIM)
    done = []
    for side in range(2):
        base = side * rows
        for edge in range(2):
            begin = base + edge * (rows - RIM)
            at = slice(begin, begin + RIM)
            kv = kv_all[at].astype(jnp.bfloat16)
            more = attend(query[at], kv[:, :width], kv[:, width:], rim)
            place = slice((edge * 2 + side) * RIM, (edge * 2 + side + 1) * RIM)
            store(rim_ref, place, more if rim_before is None else add_keys(load(rim_before, place), more))
        at = slice(base + RIM, base + rows - RIM)
        kv = kv_all[at].astype(jnp.bfloat16)
        more = attend(query[at], kv[:, :width], kv[:, width:], inner)
        place = slice(side * count, (side + 1) * count)
        if inner_before is None:
            store(inner_ref, place, more)
        else:
            done.append(add_keys(load(inner_before, place), more))
    return done


def pack_kernel(ready_ref, *refs):
    *parts, south_ref, north_ref = refs
    rows = parts[0].shape[0]
    for i, part in enumerate(parts):
        values = part[...].astype(jnp.float32)
        south_ref[i] = values[:RIM].astype(jnp.bfloat16)
        north_ref[i] = values[rows - RIM :].astype(jnp.bfloat16)


def halo_kernel(
    query_ref, inner_ref, rim_ref, own_w_ref, own_e_ref, west_ref, east_ref, gain_ref, qkv_ref, out_w_ref, out_ref, rim_out_ref
):
    width = west_ref.shape[-1]
    rows = west_ref.shape[0]
    halos = jnp.concatenate([r[...].astype(jnp.float32) for r in (west_ref, east_ref)], axis=0)
    halos = matmul(layer_norm(halos, gain_ref[...]), qkv_ref[:, width:])
    done = add_halves(query_ref[...], halos, None, rim_out_ref, inner_ref, rim_ref)
    done = tuple(jnp.concatenate(p, axis=0) for p in zip(*done))
    tokens = [r[...].astype(jnp.float32)[RIM : rows - RIM] for r in (own_w_ref, own_e_ref)]
    out_ref[...] = project(jnp.concatenate(tokens, axis=0), done, out_w_ref)


def add_rims(closed_ref, query_ref, rim_ref, north_ref, south_ref, gain_ref, qkv_ref):
    width = query_ref.shape[-1]
    rows = query_ref.shape[0] // 2
    beyond = jnp.concatenate([r[p].astype(jnp.float32) for r in (north_ref, south_ref) for p in range(4)], axis=0)
    beyond = matmul(layer_norm(beyond, gain_ref[...]), qkv_ref[:, width:])
    rim = level_bias(RIM, 2 * RIM)
    done = []
    for edge in range(2):
        for side in range(2):
            begin = side * rows + edge * (rows - RIM)
            place = slice((edge * 2 + side) * RIM, (edge * 2 + side + 1) * RIM)
            first, second = ((edge * 4 + part) * RIM for part in (side, side + 2))
            kv = jnp.concatenate([beyond[first : first + RIM], beyond[second : second + RIM]], axis=0)
            kv = kv.astype(jnp.bfloat16)
            query = query_ref[begin : begin + RIM]
            more = attend(query, kv[:, :width], kv[:, width:], rim + closed_ref[edge])
            done.append(add_keys(load(rim_ref, place), more))
    return done


def corner_kernel(
    closed_ref,
    query_ref,
    rim_ref,
    north_ref,
    south_ref,
    gain_ref,
    qkv_ref,
    own_w_ref,
    own_e_ref,
    middle_ref,
    out_w_ref,
    out_ref,
):
    rows = own_w_ref.shape[0]
    done = add_rims(closed_ref, query_ref, rim_ref, north_ref, south_ref, gain_ref, qkv_ref)
    done = tuple(jnp.concatenate(p, axis=0) for p in zip(*done))
    own = [r[...].astype(jnp.float32) for r in (own_w_ref, own_e_ref)]
    tokens = [half[at] for at in (slice(0, RIM), slice(rows - RIM, rows)) for half in own]
    mixed = project(jnp.concatenate(tokens, axis=0), done, out_w_ref).astype(jnp.float32)
    middle = middle_ref[...].astype(jnp.float32)
    count = rows - 2 * RIM
    for side in range(2):
        out_ref[side] = jnp.concatenate(
            [
                mixed[side * RIM : (side + 1) * RIM],
                middle[side * count : (side + 1) * count],
                mixed[(2 + side) * RIM : (3 + side) * RIM],
            ],
            axis=0,
        ).astype(jnp.bfloat16)


def call(kernel, results, flops, *operands):
    moved = sum(x.size * x.dtype.itemsize for x in (*operands, *results))
    specs = [pl.BlockSpec(memory_space=pltpu.SMEM if x.ndim == 1 else pltpu.VMEM) for x in operands]
    return pl.pallas_call(
        kernel,
        out_shape=results,
        in_specs=specs,
        out_specs=[pl.BlockSpec(memory_space=pltpu.VMEM)] * len(results),
        compiler_params=pltpu.CompilerParams(vmem_limit_bytes=14 * 2**20),
        cost_estimate=pl.CostEstimate(flops=flops, bytes_accessed=moved, transcendentals=0),
    )(*operands)


def shards(tokens, gain_attn, weight_qkv, weight_out):
    lev_count, row_count, col_count, width = tokens.shape
    rows = row_count * HALF * lev_count
    by_place = tokens.transpose(1, 2, 0, 3)
    own_w = by_place[:, :HALF].reshape(rows, width)
    own_e = by_place[:, HALF:].reshape(rows, width)
    east = shift(own_w, "lon", -1, True)
    west = shift(own_e, "lon", 1, True)
    gain = gain_attn.reshape(1, width)
    place = lax.axis_index("lat")
    closed = jnp.stack([place == 0, place == lax.axis_size("lat") - 1])
    closed = jnp.where(closed, FAR, 0.0).astype(jnp.float32)

    def shape(*dims, dtype=jnp.float32):
        return jax.ShapeDtypeStruct(dims, dtype)

    inner_shape = shape(3, 2 * (rows - 2 * RIM), width)
    rim_shape = shape(3, 4 * RIM, width)
    query, inner, rim, ready = call(
        own_kernel,
        [shape(2 * rows, width), inner_shape, rim_shape, shape(8, 128)],
        2_000_000_000,
        own_w,
        own_e,
        gain,
        weight_qkv,
    )
    packed = shape(4, RIM, width, dtype=jnp.bfloat16)
    to_south, to_north = call(pack_kernel, [packed, packed], 1_000_000, ready, own_w, own_e, west, east)
    far_south = shift(to_south, "lat", -1, False)
    far_north = shift(to_north, "lat", 1, False)
    middle, rim = call(
        halo_kernel,
        [shape(2 * (rows - 2 * RIM), width, dtype=jnp.bfloat16), rim_shape],
        1_500_000_000,
        query,
        inner,
        rim,
        own_w,
        own_e,
        west,
        east,
        gain,
        weight_qkv,
        weight_out,
    )
    (mixed,) = call(
        corner_kernel,
        [shape(2, rows, width, dtype=jnp.bfloat16)],
        1_000_000_000,
        closed,
        query,
        rim,
        far_north,
        far_south,
        gain,
        weight_qkv,
        own_w,
        own_e,
        middle,
        weight_out,
    )
    mixed = mixed.reshape(2, row_count, HALF, lev_count, width).transpose(1, 0, 2, 3, 4)
    return mixed.reshape(row_count, col_count, lev_count, width).transpose(2, 0, 1, 3)


def solution(mesh):
    placed = (P(None, "lat", "lon", None), P(), P(), P())
    return jax.shard_map(
        shards, mesh=mesh, in_specs=placed, out_specs=P(None, "lat", "lon", None), check_vma=False
    )
```

```python
import jax
import jax.numpy as jnp
from jax import lax
from jax.experimental import pallas as pl
from jax.experimental.pallas import tpu as pltpu
from jax.sharding import PartitionSpec as P

HEADS = 8
HEAD_SIZE = 64
GROUP = 4
SPAN = GROUP * HEAD_SIZE
EPS = 1e-05
FAR = -1e30
HALF = 6
EDGE = 3
LEVELS = 4
RIM = EDGE * HALF * LEVELS


def shift(value, axis, by, wrap):
    count = lax.axis_size(axis)
    pairs = [(i, (i + by) % count) for i in range(count) if wrap or 0 <= i + by < count]
    return lax.ppermute(value, axis, pairs)


def layer_norm(values, gain):
    center = values - jnp.mean(values, axis=-1, keepdims=True)
    spread = jnp.mean(center * center, axis=-1, keepdims=True)
    return (center * lax.rsqrt(spread + EPS) * gain).astype(jnp.bfloat16)


def matmul(a, b):
    return jnp.dot(a, b, preferred_element_type=jnp.float32)


def rounded(values):
    return values.astype(jnp.bfloat16).astype(jnp.float32)


def level_bias(rows, keys):
    def part(axis):
        level = lax.broadcasted_iota(jnp.int32, (rows, keys), axis) % LEVELS
        return jnp.where(level == 0, 2, jnp.where(level == LEVELS - 1, 1, 0))

    return jnp.where(part(0) == part(1), 0.0, FAR).astype(jnp.float32)


def attend(query, keys, values, bias):
    rows = query.shape[0]
    owner = lax.broadcasted_iota(jnp.int32, (rows, SPAN), 1) // HEAD_SIZE
    tall = jnp.concatenate([bias] * GROUP, axis=0)
    parts = []
    for start in range(0, query.shape[1], SPAN):
        piece = query[:, start : start + SPAN]
        spread = jnp.concatenate(
            [jnp.where(owner == h, piece, 0.0) for h in range(GROUP)], axis=0
        ).astype(jnp.bfloat16)
        scores = lax.dot_general(
            spread,
            keys[:, start : start + SPAN],
            (((1,), (1,)), ((), ())),
            preferred_element_type=jnp.float32,
        )
        scores = scores + tall
        expo = jnp.exp(scores - jnp.max(scores, axis=-1, keepdims=True))
        scale = 1.0 / jnp.sum(expo, axis=-1, keepdims=True)
        out = matmul(expo.astype(jnp.bfloat16), values[:, start : start + SPAN]) * scale
        merged = out[:rows]
        for h in range(1, GROUP):
            merged = jnp.where(owner == h, out[h * rows : (h + 1) * rows], merged)
        parts.append(merged)
    return jnp.concatenate(parts, axis=1)


def project(tokens, heads, weight_ref):
    branch = matmul(heads.astype(jnp.bfloat16), weight_ref[...])
    return (tokens + rounded(branch)).astype(jnp.bfloat16)


def make_query(normed, qkv_ref):
    width = normed.shape[-1]
    return rounded(matmul(normed, qkv_ref[:, :width])) * HEAD_SIZE**-0.5


def make_keys(normed, qkv_ref):
    width = normed.shape[-1]
    return matmul(normed, qkv_ref[:, width:])


def inner_kernel(
    own_w_ref,
    own_e_ref,
    west_ref,
    east_ref,
    gain_ref,
    qkv_ref,
    out_w_ref,
    out_ref,
    query_ref,
    keys_ref,
):
    rows, width = own_w_ref.shape
    count = rows - 2 * RIM
    gain = gain_ref[...]
    own = jnp.concatenate([r[...].astype(jnp.float32) for r in (own_w_ref, own_e_ref)], axis=0)
    normed = layer_norm(own, gain)
    query = make_query(normed, qkv_ref)
    mine = make_keys(normed, qkv_ref)
    halos = jnp.concatenate([r[...].astype(jnp.float32) for r in (west_ref, east_ref)], axis=0)
    halos = make_keys(layer_norm(halos, gain), qkv_ref)
    for edge in range(2):
        for side in range(2):
            place = edge * 2 + side
            begin = side * rows + edge * (rows - RIM)
            at = slice(begin, begin + RIM)
            query_ref[place] = query[at]
            keys_ref[place] = jnp.concatenate([mine[at], halos[at]], axis=0).astype(jnp.bfloat16)
    bias = level_bias(count, 2 * count)
    heads, tokens = [], []
    for side in range(2):
        at = slice(side * rows + RIM, (side + 1) * rows - RIM)
        kv = jnp.concatenate([mine[at], halos[at]], axis=0).astype(jnp.bfloat16)
        heads.append(attend(query[at], kv[:, :width], kv[:, width:], bias))
        tokens.append(own[at])
    out_ref[...] = project(jnp.concatenate(tokens, axis=0), jnp.concatenate(heads, axis=0), out_w_ref)


def edge_kernel(
    closed_ref,
    query_ref,
    keys_ref,
    north_ref,
    south_ref,
    far_north_ref,
    far_south_ref,
    own_w_ref,
    own_e_ref,
    middle_ref,
    gain_ref,
    qkv_ref,
    out_w_ref,
    out_ref,
):
    rows, width = own_w_ref.shape
    count = rows - 2 * RIM
    refs = ((north_ref, far_north_ref), (south_ref, far_south_ref))
    beyond = [r[side].astype(jnp.float32) for pair in refs for side in range(2) for r in pair]
    beyond = make_keys(layer_norm(jnp.concatenate(beyond, axis=0), gain_ref[...]), qkv_ref).astype(jnp.bfloat16)
    levels = level_bias(RIM, 4 * RIM)
    distant = lax.broadcasted_iota(jnp.int32, (RIM, 4 * RIM), 1) >= 2 * RIM
    own = [r[...].astype(jnp.float32) for r in (own_w_ref, own_e_ref)]
    heads, tokens = [], []
    for edge in range(2):
        bias = levels + jnp.where(distant, closed_ref[edge], 0.0)
        for side in range(2):
            place = edge * 2 + side
            begin = edge * (rows - RIM)
            kv = jnp.concatenate([keys_ref[place], beyond[2 * place * RIM : 2 * (place + 1) * RIM]], axis=0)
            heads.append(attend(query_ref[place], kv[:, :width], kv[:, width:], bias))
            tokens.append(own[side][begin : begin + RIM])
    mixed = project(jnp.concatenate(tokens, axis=0), jnp.concatenate(heads, axis=0), out_w_ref).astype(jnp.float32)
    middle = middle_ref[...].astype(jnp.float32)
    for side in range(2):
        out_ref[side] = jnp.concatenate(
            [
                mixed[side * RIM : (side + 1) * RIM],
                middle[side * count : (side + 1) * count],
                mixed[(2 + side) * RIM : (3 + side) * RIM],
            ],
            axis=0,
        ).astype(jnp.bfloat16)


def call(kernel, results, flops, *operands):
    moved = sum(x.size * x.dtype.itemsize for x in (*operands, *results))
    specs = [pl.BlockSpec(memory_space=pltpu.SMEM if x.ndim == 1 else pltpu.VMEM) for x in operands]
    return pl.pallas_call(
        kernel,
        out_shape=results,
        in_specs=specs,
        out_specs=[pl.BlockSpec(memory_space=pltpu.VMEM)] * len(results),
        compiler_params=pltpu.CompilerParams(vmem_limit_bytes=14 * 2**20),
        cost_estimate=pl.CostEstimate(flops=flops, bytes_accessed=moved, transcendentals=0),
    )(*operands)


def shards(tokens, gain_attn, weight_qkv, weight_out):
    lev_count, row_count, col_count, width = tokens.shape
    rows = row_count * HALF * lev_count
    by_place = tokens.transpose(1, 2, 0, 3)
    own_w = by_place[:, :HALF].reshape(rows, width)
    own_e = by_place[:, HALF:].reshape(rows, width)
    east = shift(own_w, "lon", -1, True)
    west = shift(own_e, "lon", 1, True)

    def rim(*halves):
        return jnp.stack([h[:RIM] for h in halves]), jnp.stack([h[rows - RIM :] for h in halves])

    first, last = rim(own_w, own_e)
    south = shift(first, "lat", -1, False)
    north = shift(last, "lat", 1, False)
    first, last = rim(west, east)
    far_south = shift(first, "lat", -1, False)
    far_north = shift(last, "lat", 1, False)
    gain = gain_attn.reshape(1, width)
    place = lax.axis_index("lat")
    closed = jnp.stack([place == 0, place == lax.axis_size("lat") - 1])
    closed = jnp.where(closed, FAR, 0.0).astype(jnp.float32)

    def shape(*dims, dtype=jnp.float32):
        return jax.ShapeDtypeStruct(dims, dtype)

    middle, query, keys = call(
        inner_kernel,
        [
            shape(2 * (rows - 2 * RIM), width, dtype=jnp.bfloat16),
            shape(4, RIM, width),
            shape(4, 2 * RIM, 2 * width, dtype=jnp.bfloat16),
        ],
        2_500_000_000,
        own_w,
        own_e,
        west,
        east,
        gain,
        weight_qkv,
        weight_out,
    )
    (mixed,) = call(
        edge_kernel,
        [shape(2, rows, width, dtype=jnp.bfloat16)],
        1_000_000_000,
        closed,
        query,
        keys,
        north,
        south,
        far_north,
        far_south,
        own_w,
        own_e,
        middle,
        gain,
        weight_qkv,
        weight_out,
    )
    mixed = mixed.reshape(2, row_count, HALF, lev_count, width).transpose(1, 0, 2, 3, 4)
    return mixed.reshape(row_count, col_count, lev_count, width).transpose(2, 0, 1, 3)


def solution(mesh):
    placed = (P(None, "lat", "lon", None), P(), P(), P())
    return jax.shard_map(
        shards, mesh=mesh, in_specs=placed, out_specs=P(None, "lat", "lon", None), check_vma=False
    )
```

```python
import jax
import jax.numpy as jnp
from jax import lax
from jax.experimental import pallas as pl
from jax.experimental.pallas import tpu as pltpu
from jax.sharding import PartitionSpec as P

HEADS = 8
HEAD_SIZE = 64
GROUP = 4
SPAN = GROUP * HEAD_SIZE
EPS = 1e-05
FAR = -1e30
HALF = 6
EDGE = 3
LEVELS = 4
RIM = EDGE * HALF * LEVELS


def shift(value, axis, by, wrap):
    count = lax.axis_size(axis)
    pairs = [(i, (i + by) % count) for i in range(count) if wrap or 0 <= i + by < count]
    return lax.ppermute(value, axis, pairs)


def layer_norm(values, gain):
    center = values - jnp.mean(values, axis=-1, keepdims=True)
    spread = jnp.mean(center * center, axis=-1, keepdims=True)
    return (center * lax.rsqrt(spread + EPS) * gain).astype(jnp.bfloat16)


def matmul(a, b):
    return jnp.dot(a, b, preferred_element_type=jnp.float32)


def rounded(values):
    return values.astype(jnp.bfloat16).astype(jnp.float32)


def level_bias(rows, keys):
    def part(axis):
        level = lax.broadcasted_iota(jnp.int32, (rows, keys), axis) & (LEVELS - 1)
        return jnp.where(level == 0, 2, jnp.where(level == LEVELS - 1, 1, 0))

    return jnp.where(part(0) == part(1), 0.0, FAR).astype(jnp.float32)


def attend(query, keys, values, bias):
    rows = query.shape[0]
    owner = lax.broadcasted_iota(jnp.int32, (rows, SPAN), 1) >> 6
    tall = jnp.concatenate([bias] * GROUP, axis=0)
    parts = []
    for start in range(0, query.shape[1], SPAN):
        piece = query[:, start : start + SPAN]
        spread = jnp.concatenate(
            [jnp.where(owner == h, piece, 0.0) for h in range(GROUP)], axis=0
        ).astype(jnp.bfloat16)
        scores = lax.dot_general(
            spread,
            keys[:, start : start + SPAN],
            (((1,), (1,)), ((), ())),
            preferred_element_type=jnp.float32,
        )
        scores = scores + tall
        expo = jnp.exp(scores - jnp.max(scores, axis=-1, keepdims=True))
        scale = 1.0 / jnp.sum(expo, axis=-1, keepdims=True)
        out = matmul(expo.astype(jnp.bfloat16), values[:, start : start + SPAN]) * scale
        merged = out[:rows]
        for h in range(1, GROUP):
            merged = jnp.where(owner == h, out[h * rows : (h + 1) * rows], merged)
        parts.append(merged)
    return jnp.concatenate(parts, axis=1)


def project(tokens, heads, weight_ref):
    branch = matmul(heads.astype(jnp.bfloat16), weight_ref[...])
    return (tokens + rounded(branch)).astype(jnp.bfloat16)


def make_query(normed, qkv_ref):
    width = normed.shape[-1]
    return rounded(matmul(normed, qkv_ref[:, :width])) * HEAD_SIZE**-0.5


def make_keys(normed, qkv_ref):
    width = normed.shape[-1]
    return matmul(normed, qkv_ref[:, width:])


def inner_kernel(
    own_w_ref,
    own_e_ref,
    west_ref,
    east_ref,
    gain_ref,
    qkv_ref,
    out_w_ref,
    out_ref,
    query_ref,
    keys_ref,
):
    rows, width = own_w_ref.shape
    count = rows - 2 * RIM
    gain = gain_ref[...]
    own = jnp.concatenate([r[...].astype(jnp.float32) for r in (own_w_ref, own_e_ref)], axis=0)
    normed = layer_norm(own, gain)
    query = make_query(normed, qkv_ref)
    mine = make_keys(normed, qkv_ref)
    halos = jnp.concatenate([r[...].astype(jnp.float32) for r in (west_ref, east_ref)], axis=0)
    halos = make_keys(layer_norm(halos, gain), qkv_ref)
    for edge in range(2):
        for side in range(2):
            place = edge * 2 + side
            begin = side * rows + edge * (rows - RIM)
            at = slice(begin, begin + RIM)
            query_ref[place] = query[at]
            keys_ref[place] = jnp.concatenate([mine[at], halos[at]], axis=0).astype(jnp.bfloat16)
    bias = level_bias(count, 2 * count)
    heads, tokens = [], []
    for side in range(2):
        at = slice(side * rows + RIM, (side + 1) * rows - RIM)
        kv = jnp.concatenate([mine[at], halos[at]], axis=0).astype(jnp.bfloat16)
        heads.append(attend(query[at], kv[:, :width], kv[:, width:], bias))
        tokens.append(own[at])
    out_ref[...] = project(jnp.concatenate(tokens, axis=0), jnp.concatenate(heads, axis=0), out_w_ref)


def edge_kernel(
    closed_ref,
    query_ref,
    keys_ref,
    north_ref,
    south_ref,
    own_w_ref,
    own_e_ref,
    middle_ref,
    gain_ref,
    qkv_ref,
    out_w_ref,
    out_ref,
):
    rows, width = own_w_ref.shape
    count = rows - 2 * RIM
    beyond = [r[part].astype(jnp.float32) for r in (north_ref, south_ref) for part in range(4)]
    beyond = make_keys(layer_norm(jnp.concatenate(beyond, axis=0), gain_ref[...]), qkv_ref).astype(jnp.bfloat16)
    levels = level_bias(RIM, 4 * RIM)
    distant = lax.broadcasted_iota(jnp.int32, (RIM, 4 * RIM), 1) >= 2 * RIM
    own = [r[...].astype(jnp.float32) for r in (own_w_ref, own_e_ref)]
    heads, tokens = [], []
    for edge in range(2):
        bias = levels + jnp.where(distant, closed_ref[edge], 0.0)
        for side in range(2):
            place = edge * 2 + side
            begin = edge * (rows - RIM)
            kv = jnp.concatenate([keys_ref[place], beyond[2 * place * RIM : 2 * (place + 1) * RIM]], axis=0)
            heads.append(attend(query_ref[place], kv[:, :width], kv[:, width:], bias))
            tokens.append(own[side][begin : begin + RIM])
    mixed = project(jnp.concatenate(tokens, axis=0), jnp.concatenate(heads, axis=0), out_w_ref).astype(jnp.float32)
    middle = middle_ref[...].astype(jnp.float32)
    for side in range(2):
        half = jnp.concatenate(
            [
                mixed[side * RIM : (side + 1) * RIM],
                middle[side * count : (side + 1) * count],
                mixed[(2 + side) * RIM : (3 + side) * RIM],
            ],
            axis=0,
        )
        half = half.reshape(rows // (HALF * LEVELS), HALF, LEVELS, width).astype(jnp.bfloat16)
        out_ref[:, side * HALF : (side + 1) * HALF] = half


def call(kernel, results, flops, *operands):
    moved = sum(x.size * x.dtype.itemsize for x in (*operands, *results))
    specs = [pl.BlockSpec(memory_space=pltpu.SMEM if x.ndim == 1 else pltpu.VMEM) for x in operands]
    return pl.pallas_call(
        kernel,
        out_shape=results,
        in_specs=specs,
        out_specs=[pl.BlockSpec(memory_space=pltpu.VMEM)] * len(results),
        compiler_params=pltpu.CompilerParams(vmem_limit_bytes=14 * 2**20),
        cost_estimate=pl.CostEstimate(flops=flops, bytes_accessed=moved, transcendentals=0),
    )(*operands)


def shards(tokens, gain_attn, weight_qkv, weight_out):
    lev_count, row_count, col_count, width = tokens.shape
    rows = row_count * HALF * lev_count
    by_place = tokens.transpose(1, 2, 0, 3)
    own_w = by_place[:, :HALF].reshape(rows, width)
    own_e = by_place[:, HALF:].reshape(rows, width)
    east = shift(own_w, "lon", -1, True)
    west = shift(own_e, "lon", 1, True)

    def rim(*halves):
        return jnp.stack([h[:RIM] for h in halves]), jnp.stack([h[rows - RIM :] for h in halves])

    first, last = rim(own_w, west, own_e, east)
    south = shift(first, "lat", -1, False)
    north = shift(last, "lat", 1, False)
    gain = gain_attn.reshape(1, width)
    place = lax.axis_index("lat")
    closed = jnp.stack([place == 0, place == lax.axis_size("lat") - 1])
    closed = jnp.where(closed, FAR, 0.0).astype(jnp.float32)

    def shape(*dims, dtype=jnp.float32):
        return jax.ShapeDtypeStruct(dims, dtype)

    middle, query, keys = call(
        inner_kernel,
        [
            shape(2 * (rows - 2 * RIM), width, dtype=jnp.bfloat16),
            shape(4, RIM, width),
            shape(4, 2 * RIM, 2 * width, dtype=jnp.bfloat16),
        ],
        2_500_000_000,
        own_w,
        own_e,
        west,
        east,
        gain,
        weight_qkv,
        weight_out,
    )
    (mixed,) = call(
        edge_kernel,
        [shape(row_count, col_count, lev_count, width, dtype=jnp.bfloat16)],
        1_000_000_000,
        closed,
        query,
        keys,
        north,
        south,
        own_w,
        own_e,
        middle,
        gain,
        weight_qkv,
        weight_out,
    )
    return mixed.transpose(2, 0, 1, 3)


def solution(mesh):
    placed = (P(None, "lat", "lon", None), P(), P(), P())
    return jax.shard_map(
        shards, mesh=mesh, in_specs=placed, out_specs=P(None, "lat", "lon", None), check_vma=False
    )
```

```python
import jax
import jax.numpy as jnp
from jax import lax
from jax.experimental import pallas as pl
from jax.experimental.pallas import tpu as pltpu
from jax.sharding import PartitionSpec as P

HEADS = 8
HEAD_SIZE = 64
GROUP = 4
SPAN = GROUP * HEAD_SIZE
EPS = 1e-05
FAR = -1e30
HALF = 6
EDGE = 3
LEVELS = 4
RIM = EDGE * HALF * LEVELS


def shift(value, axis, by, wrap):
    count = lax.axis_size(axis)
    pairs = [(i, (i + by) % count) for i in range(count) if wrap or 0 <= i + by < count]
    return lax.ppermute(value, axis, pairs)


def layer_norm(values, gain):
    center = values - jnp.mean(values, axis=-1, keepdims=True)
    spread = jnp.mean(center * center, axis=-1, keepdims=True)
    return (center * lax.rsqrt(spread + EPS) * gain).astype(jnp.bfloat16)


def matmul(a, b):
    return jnp.dot(a, b, preferred_element_type=jnp.float32)


def rounded(values):
    return values.astype(jnp.bfloat16).astype(jnp.float32)


def level_bias(rows, keys):
    def part(axis):
        level = lax.broadcasted_iota(jnp.int32, (rows, keys), axis) & (LEVELS - 1)
        return jnp.where(level == 0, 2, jnp.where(level == LEVELS - 1, 1, 0))

    return jnp.where(part(0) == part(1), 0.0, FAR).astype(jnp.float32)


def attend(query, keys, values, bias):
    rows = query.shape[0]
    owner = lax.broadcasted_iota(jnp.int32, (rows, SPAN), 1) >> 6
    tall = jnp.concatenate([bias] * GROUP, axis=0)
    parts = []
    for start in range(0, query.shape[1], SPAN):
        piece = query[:, start : start + SPAN]
        spread = jnp.concatenate(
            [jnp.where(owner == h, piece, 0.0) for h in range(GROUP)], axis=0
        ).astype(jnp.bfloat16)
        scores = lax.dot_general(
            spread,
            keys[:, start : start + SPAN],
            (((1,), (1,)), ((), ())),
            preferred_element_type=jnp.float32,
        )
        scores = scores + tall
        expo = jnp.exp(scores - jnp.max(scores, axis=-1, keepdims=True))
        scale = 1.0 / jnp.sum(expo, axis=-1, keepdims=True)
        out = matmul(expo.astype(jnp.bfloat16), values[:, start : start + SPAN]) * scale
        merged = out[:rows]
        for h in range(1, GROUP):
            merged = jnp.where(owner == h, out[h * rows : (h + 1) * rows], merged)
        parts.append(merged)
    return jnp.concatenate(parts, axis=1)


def project(tokens, heads, weight_ref):
    branch = matmul(heads.astype(jnp.bfloat16), weight_ref[...])
    return tokens + rounded(branch)


def make_query(normed, qkv_ref):
    width = normed.shape[-1]
    return rounded(matmul(normed, qkv_ref[:, :width])) * HEAD_SIZE**-0.5


def make_keys(normed, qkv_ref):
    width = normed.shape[-1]
    return matmul(normed, qkv_ref[:, width:])


def inner_kernel(
    own_w_ref,
    own_e_ref,
    west_ref,
    east_ref,
    gain_ref,
    qkv_ref,
    out_w_ref,
    out_ref,
    query_ref,
    keys_ref,
):
    rows, width = own_w_ref.shape
    count = rows - 2 * RIM
    gain = gain_ref[...]
    own = jnp.concatenate([r[...].astype(jnp.float32) for r in (own_w_ref, own_e_ref)], axis=0)
    normed = layer_norm(own, gain)
    query = make_query(normed, qkv_ref)
    mine = make_keys(normed, qkv_ref)
    halos = jnp.concatenate([r[...].astype(jnp.float32) for r in (west_ref, east_ref)], axis=0)
    halos = make_keys(layer_norm(halos, gain), qkv_ref)
    for edge in range(2):
        for side in range(2):
            place = edge * 2 + side
            begin = side * rows + edge * (rows - RIM)
            at = slice(begin, begin + RIM)
            query_ref[place] = query[at]
            keys_ref[place] = jnp.concatenate([mine[at], halos[at]], axis=0).astype(jnp.bfloat16)
    bias = level_bias(count, 2 * count)
    heads, tokens = [], []
    for side in range(2):
        at = slice(side * rows + RIM, (side + 1) * rows - RIM)
        kv = jnp.concatenate([mine[at], halos[at]], axis=0).astype(jnp.bfloat16)
        heads.append(attend(query[at], kv[:, :width], kv[:, width:], bias))
        tokens.append(own[at])
    mixed = project(jnp.concatenate(tokens, axis=0), jnp.concatenate(heads, axis=0), out_w_ref)
    for side in range(2):
        place_half(out_ref, slice(None), side, mixed[side * count : (side + 1) * count])


def place_half(out_ref, at, side, half):
    half = half.reshape(-1, HALF, LEVELS, half.shape[-1]).astype(jnp.bfloat16)
    out_ref[at, side * HALF : (side + 1) * HALF] = half


def latitude_kernel(north_ref, south_ref, gain_ref, qkv_ref, keys_ref):
    beyond = jnp.concatenate([r[s].astype(jnp.float32) for r in (north_ref, south_ref) for s in range(2)], axis=0)
    beyond = make_keys(layer_norm(beyond, gain_ref[...]), qkv_ref)
    for place in range(4):
        keys_ref[place] = beyond[place * RIM : (place + 1) * RIM]


def edge_kernel(
    closed_ref,
    query_ref,
    keys_ref,
    beyond_ref,
    north_ref,
    south_ref,
    own_w_ref,
    own_e_ref,
    middle_ref,
    gain_ref,
    qkv_ref,
    out_w_ref,
    out_ref,
):
    rows, width = own_w_ref.shape
    corners = jnp.concatenate([r[s].astype(jnp.float32) for r in (north_ref, south_ref) for s in range(2)], axis=0)
    corners = make_keys(layer_norm(corners, gain_ref[...]), qkv_ref)
    levels = level_bias(RIM, 4 * RIM)
    distant = lax.broadcasted_iota(jnp.int32, (RIM, 4 * RIM), 1) >= 2 * RIM
    own = [r[...].astype(jnp.float32) for r in (own_w_ref, own_e_ref)]
    heads, tokens = [], []
    for edge in range(2):
        bias = levels + jnp.where(distant, closed_ref[edge], 0.0)
        for side in range(2):
            place = edge * 2 + side
            begin = edge * (rows - RIM)
            outer = jnp.concatenate([beyond_ref[place], corners[place * RIM : (place + 1) * RIM]], axis=0)
            kv = jnp.concatenate([keys_ref[place], outer.astype(jnp.bfloat16)], axis=0)
            heads.append(attend(query_ref[place], kv[:, :width], kv[:, width:], bias))
            tokens.append(own[side][begin : begin + RIM])
    mixed = project(jnp.concatenate(tokens, axis=0), jnp.concatenate(heads, axis=0), out_w_ref)
    out_ref[EDGE : out_ref.shape[0] - EDGE] = middle_ref[...]
    for edge in range(2):
        at = slice(0, EDGE) if edge == 0 else slice(out_ref.shape[0] - EDGE, out_ref.shape[0])
        for side in range(2):
            place = edge * 2 + side
            place_half(out_ref, at, side, mixed[place * RIM : (place + 1) * RIM])


def call(kernel, results, flops, *operands):
    moved = sum(x.size * x.dtype.itemsize for x in (*operands, *results))
    specs = [pl.BlockSpec(memory_space=pltpu.SMEM if x.ndim == 1 else pltpu.VMEM) for x in operands]
    return pl.pallas_call(
        kernel,
        out_shape=results,
        in_specs=specs,
        out_specs=[pl.BlockSpec(memory_space=pltpu.VMEM)] * len(results),
        compiler_params=pltpu.CompilerParams(vmem_limit_bytes=14 * 2**20),
        cost_estimate=pl.CostEstimate(flops=flops, bytes_accessed=moved, transcendentals=0),
    )(*operands)


def shards(tokens, gain_attn, weight_qkv, weight_out):
    lev_count, row_count, col_count, width = tokens.shape
    rows = row_count * HALF * lev_count
    by_place = tokens.transpose(1, 2, 0, 3)
    own_w = by_place[:, :HALF].reshape(rows, width)
    own_e = by_place[:, HALF:].reshape(rows, width)
    east = shift(own_w, "lon", -1, True)
    west = shift(own_e, "lon", 1, True)

    def rim(*halves):
        return jnp.stack([h[:RIM] for h in halves]), jnp.stack([h[rows - RIM :] for h in halves])

    first, last = rim(own_w, own_e)
    south = shift(first, "lat", -1, False)
    north = shift(last, "lat", 1, False)
    first, last = rim(west, east)
    far_south = shift(first, "lat", -1, False)
    far_north = shift(last, "lat", 1, False)
    gain = gain_attn.reshape(1, width)
    place = lax.axis_index("lat")
    closed = jnp.stack([place == 0, place == lax.axis_size("lat") - 1])
    closed = jnp.where(closed, FAR, 0.0).astype(jnp.float32)

    def shape(*dims, dtype=jnp.float32):
        return jax.ShapeDtypeStruct(dims, dtype)

    middle, query, keys = call(
        inner_kernel,
        [
            shape(row_count - 2 * EDGE, col_count, lev_count, width, dtype=jnp.bfloat16),
            shape(4, RIM, width),
            shape(4, 2 * RIM, 2 * width, dtype=jnp.bfloat16),
        ],
        2_500_000_000,
        own_w,
        own_e,
        west,
        east,
        gain,
        weight_qkv,
        weight_out,
    )
    (beyond,) = call(latitude_kernel, [shape(4, RIM, 2 * width)], 300_000_000, north, south, gain, weight_qkv)
    (mixed,) = call(
        edge_kernel,
        [shape(row_count, col_count, lev_count, width, dtype=jnp.bfloat16)],
        1_000_000_000,
        closed,
        query,
        keys,
        beyond,
        far_north,
        far_south,
        own_w,
        own_e,
        middle,
        gain,
        weight_qkv,
        weight_out,
    )
    return mixed.transpose(2, 0, 1, 3)


def solution(mesh):
    placed = (P(None, "lat", "lon", None), P(), P(), P())
    return jax.shard_map(
        shards, mesh=mesh, in_specs=placed, out_specs=P(None, "lat", "lon", None), check_vma=False
    )
```

```python
import jax
import jax.numpy as jnp
from jax import lax
from jax.experimental import pallas as pl
from jax.experimental.pallas import tpu as pltpu
from jax.sharding import PartitionSpec as P

HEADS = 8
HEAD_SIZE = 64
GROUP = 4
SPAN = GROUP * HEAD_SIZE
EPS = 1e-05
FAR = -1e30
HALF = 6
EDGE = 3
LEVELS = 4
RIM = EDGE * HALF * LEVELS


def shift(value, axis, by, wrap):
    count = lax.axis_size(axis)
    pairs = [(i, (i + by) % count) for i in range(count) if wrap or 0 <= i + by < count]
    return lax.ppermute(value, axis, pairs)


def layer_norm(values, gain):
    center = values - jnp.mean(values, axis=-1, keepdims=True)
    spread = jnp.mean(center * center, axis=-1, keepdims=True)
    return (center * lax.rsqrt(spread + EPS) * gain).astype(jnp.bfloat16)


def matmul(a, b):
    return jnp.dot(a, b, preferred_element_type=jnp.float32)


def rounded(values):
    return values.astype(jnp.bfloat16).astype(jnp.float32)


def level_bias(rows, keys):
    def part(axis):
        level = lax.broadcasted_iota(jnp.int32, (rows, keys), axis) & (LEVELS - 1)
        return jnp.where(level == 0, 2, jnp.where(level == LEVELS - 1, 1, 0))

    return jnp.where(part(0) == part(1), 0.0, FAR).astype(jnp.float32)


def attend(query, kv, bias):
    rows, width = query.shape
    owner = lax.broadcasted_iota(jnp.int32, (rows, SPAN), 1) >> 6
    tall = jnp.concatenate([bias] * GROUP, axis=0)

    def merge(values):
        merged = jnp.broadcast_to(values[:rows], (rows, SPAN))
        for h in range(1, GROUP):
            merged = jnp.where(owner == h, values[h * rows : (h + 1) * rows], merged)
        return merged

    parts = []
    for start in range(0, width, SPAN):
        piece = query[:, start : start + SPAN]
        spread = jnp.concatenate(
            [jnp.where(owner == h, piece, 0.0) for h in range(GROUP)], axis=0
        ).astype(jnp.bfloat16)
        scores = lax.dot_general(
            spread,
            kv[:, start : start + SPAN],
            (((1,), (1,)), ((), ())),
            preferred_element_type=jnp.float32,
        )
        scores = scores + tall
        top = jnp.max(scores, axis=-1, keepdims=True)
        expo = jnp.exp(scores - top)
        total = jnp.sum(expo, axis=-1, keepdims=True)
        out = matmul(expo.astype(jnp.bfloat16), kv[:, width + start : width + start + SPAN])
        parts.append((merge(out), merge(top), merge(total)))
    return tuple(jnp.concatenate(p, axis=1) for p in zip(*parts))


def add_keys(state, more):
    out, top, total = state
    out_2, top_2, total_2 = more
    peak = jnp.maximum(top, top_2)
    old, new = jnp.exp(top - peak), jnp.exp(top_2 - peak)
    return out * old + out_2 * new, peak, total * old + total_2 * new


def project(tokens, states, weight_ref):
    heads = [out * (1.0 / total) for out, _, total in states]
    branch = matmul(jnp.concatenate(heads, axis=0).astype(jnp.bfloat16), weight_ref[...])
    return tokens + rounded(branch)


def make_query(normed, qkv_ref):
    width = normed.shape[-1]
    return rounded(matmul(normed, qkv_ref[:, :width])) * HEAD_SIZE**-0.5


def make_keys(normed, qkv_ref):
    width = normed.shape[-1]
    return matmul(normed, qkv_ref[:, width:])


def inner_kernel(
    own_w_ref,
    own_e_ref,
    west_ref,
    east_ref,
    gain_ref,
    qkv_ref,
    out_w_ref,
    out_ref,
    query_ref,
    state_ref,
):
    rows, width = own_w_ref.shape
    count = rows - 2 * RIM
    gain = gain_ref[...]
    own = jnp.concatenate([r[...].astype(jnp.float32) for r in (own_w_ref, own_e_ref)], axis=0)
    normed = layer_norm(own, gain)
    query = make_query(normed, qkv_ref)
    halos = jnp.concatenate([r[...].astype(jnp.float32) for r in (west_ref, east_ref)], axis=0)
    kv = make_keys(jnp.concatenate([normed, layer_norm(halos, gain)], axis=0), qkv_ref)
    mine, halos = kv[: 2 * rows], kv[2 * rows :]
    rim = level_bias(RIM, 2 * RIM)
    for edge in range(2):
        for side in range(2):
            place = edge * 2 + side
            begin = side * rows + edge * (rows - RIM)
            at = slice(begin, begin + RIM)
            query_ref[place] = query[at]
            both = jnp.concatenate([mine[at], halos[at]], axis=0).astype(jnp.bfloat16)
            for i, value in enumerate(attend(query[at], both, rim)):
                state_ref[i, place] = value
    bias = level_bias(count, 2 * count)
    states, tokens = [], []
    for side in range(2):
        at = slice(side * rows + RIM, (side + 1) * rows - RIM)
        both = jnp.concatenate([mine[at], halos[at]], axis=0).astype(jnp.bfloat16)
        states.append(attend(query[at], both, bias))
        tokens.append(own[at])
    mixed = project(jnp.concatenate(tokens, axis=0), states, out_w_ref)
    for side in range(2):
        place_half(out_ref, slice(None), side, mixed[side * count : (side + 1) * count])


def place_half(out_ref, at, side, half):
    half = half.reshape(-1, HALF, LEVELS, half.shape[-1]).astype(jnp.bfloat16)
    out_ref[at, side * HALF : (side + 1) * HALF] = half


def edge_kernel(
    closed_ref,
    query_ref,
    state_ref,
    north_ref,
    south_ref,
    own_w_ref,
    own_e_ref,
    middle_ref,
    gain_ref,
    qkv_ref,
    out_w_ref,
    out_ref,
):
    rows, width = own_w_ref.shape
    beyond = [r[part].astype(jnp.float32) for r in (north_ref, south_ref) for part in range(4)]
    beyond = make_keys(layer_norm(jnp.concatenate(beyond, axis=0), gain_ref[...]), qkv_ref).astype(jnp.bfloat16)
    levels = level_bias(RIM, 2 * RIM)
    own = [r[...].astype(jnp.float32) for r in (own_w_ref, own_e_ref)]
    states, tokens = [], []
    for edge in range(2):
        bias = levels + closed_ref[edge]
        for side in range(2):
            place = edge * 2 + side
            begin = edge * (rows - RIM)
            more = attend(query_ref[place], beyond[2 * place * RIM : 2 * (place + 1) * RIM], bias)
            states.append(add_keys(tuple(state_ref[i, place] for i in range(3)), more))
            tokens.append(own[side][begin : begin + RIM])
    mixed = project(jnp.concatenate(tokens, axis=0), states, out_w_ref)
    out_ref[EDGE : out_ref.shape[0] - EDGE] = middle_ref[...]
    for edge in range(2):
        at = slice(0, EDGE) if edge == 0 else slice(out_ref.shape[0] - EDGE, out_ref.shape[0])
        for side in range(2):
            place = edge * 2 + side
            place_half(out_ref, at, side, mixed[place * RIM : (place + 1) * RIM])


def call(kernel, results, flops, *operands):
    moved = sum(x.size * x.dtype.itemsize for x in (*operands, *results))
    specs = [pl.BlockSpec(memory_space=pltpu.SMEM if x.ndim == 1 else pltpu.VMEM) for x in operands]
    return pl.pallas_call(
        kernel,
        out_shape=results,
        in_specs=specs,
        out_specs=[pl.BlockSpec(memory_space=pltpu.VMEM)] * len(results),
        compiler_params=pltpu.CompilerParams(vmem_limit_bytes=14 * 2**20),
        cost_estimate=pl.CostEstimate(flops=flops, bytes_accessed=moved, transcendentals=0),
    )(*operands)


def shards(tokens, gain_attn, weight_qkv, weight_out):
    lev_count, row_count, col_count, width = tokens.shape
    rows = row_count * HALF * lev_count
    by_place = tokens.transpose(1, 2, 0, 3)
    own_w = by_place[:, :HALF].reshape(rows, width)
    own_e = by_place[:, HALF:].reshape(rows, width)
    east = shift(own_w, "lon", -1, True)
    west = shift(own_e, "lon", 1, True)

    def rim(*halves):
        return jnp.stack([h[:RIM] for h in halves]), jnp.stack([h[rows - RIM :] for h in halves])

    first, last = rim(own_w, west, own_e, east)
    south = shift(first, "lat", -1, False)
    north = shift(last, "lat", 1, False)
    gain = gain_attn.reshape(1, width)
    place = lax.axis_index("lat")
    closed = jnp.stack([place == 0, place == lax.axis_size("lat") - 1])
    closed = jnp.where(closed, FAR, 0.0).astype(jnp.float32)

    def shape(*dims, dtype=jnp.float32):
        return jax.ShapeDtypeStruct(dims, dtype)

    middle, query, state = call(
        inner_kernel,
        [
            shape(row_count - 2 * EDGE, col_count, lev_count, width, dtype=jnp.bfloat16),
            shape(4, RIM, width),
            shape(3, 4, RIM, width),
        ],
        2_500_000_000,
        own_w,
        own_e,
        west,
        east,
        gain,
        weight_qkv,
        weight_out,
    )
    (mixed,) = call(
        edge_kernel,
        [shape(row_count, col_count, lev_count, width, dtype=jnp.bfloat16)],
        1_000_000_000,
        closed,
        query,
        state,
        north,
        south,
        own_w,
        own_e,
        middle,
        gain,
        weight_qkv,
        weight_out,
    )
    return mixed.transpose(2, 0, 1, 3)


def solution(mesh):
    placed = (P(None, "lat", "lon", None), P(), P(), P())
    return jax.shard_map(
        shards, mesh=mesh, in_specs=placed, out_specs=P(None, "lat", "lon", None), check_vma=False
    )
```

```python
import jax
import jax.numpy as jnp
from jax import lax
from jax.experimental import pallas as pl
from jax.experimental.pallas import tpu as pltpu
from jax.sharding import PartitionSpec as P

HEADS = 8
HEAD_SIZE = 64
GROUP = 4
SPAN = GROUP * HEAD_SIZE
EPS = 1e-05
FAR = -1e30
HALF = 6
EDGE = 3
LEVELS = 4
RIM = EDGE * HALF * LEVELS


def shift(value, axis, by, wrap):
    count = lax.axis_size(axis)
    pairs = [(i, (i + by) % count) for i in range(count) if wrap or 0 <= i + by < count]
    return lax.ppermute(value, axis, pairs)


def layer_norm(values, gain):
    center = values - jnp.mean(values, axis=-1, keepdims=True)
    spread = jnp.mean(center * center, axis=-1, keepdims=True)
    return (center * lax.rsqrt(spread + EPS) * gain).astype(jnp.bfloat16)


def matmul(a, b):
    return jnp.dot(a, b, preferred_element_type=jnp.float32)


def rounded(values):
    return values.astype(jnp.bfloat16).astype(jnp.float32)


def level_bias(rows, keys):
    def part(axis):
        level = lax.broadcasted_iota(jnp.int32, (rows, keys), axis) & (LEVELS - 1)
        return jnp.where(level == 0, 2, jnp.where(level == LEVELS - 1, 1, 0))

    return jnp.where(part(0) == part(1), 0.0, FAR).astype(jnp.float32)


def attend(query, kv, bias):
    rows, width = query.shape
    owner = lax.broadcasted_iota(jnp.int32, (rows, SPAN), 1) >> 6
    tall = jnp.concatenate([bias] * GROUP, axis=0)

    def merge(values):
        merged = jnp.broadcast_to(values[:rows], (rows, SPAN))
        for h in range(1, GROUP):
            merged = jnp.where(owner == h, values[h * rows : (h + 1) * rows], merged)
        return merged

    parts = []
    for start in range(0, width, SPAN):
        piece = query[:, start : start + SPAN]
        spread = jnp.concatenate(
            [jnp.where(owner == h, piece, 0.0) for h in range(GROUP)], axis=0
        ).astype(jnp.bfloat16)
        scores = lax.dot_general(
            spread,
            kv[:, start : start + SPAN],
            (((1,), (1,)), ((), ())),
            preferred_element_type=jnp.float32,
        )
        scores = scores + tall
        top = jnp.max(scores, axis=-1, keepdims=True)
        expo = jnp.exp(scores - top)
        total = jnp.sum(expo, axis=-1, keepdims=True)
        out = matmul(expo.astype(jnp.bfloat16), kv[:, width + start : width + start + SPAN])
        parts.append((merge(out), merge(top), merge(total)))
    return tuple(jnp.concatenate(p, axis=1) for p in zip(*parts))


def add_keys(state, more):
    out, top, total = state
    out_2, top_2, total_2 = more
    peak = jnp.maximum(top, top_2)
    old, new = jnp.exp(top - peak), jnp.exp(top_2 - peak)
    return out * old + out_2 * new, peak, total * old + total_2 * new


def project(tokens, states, weight_ref):
    heads = [out * (1.0 / total) for out, _, total in states]
    branch = matmul(jnp.concatenate(heads, axis=0).astype(jnp.bfloat16), weight_ref[...])
    return tokens + rounded(branch)


def make_query(normed, qkv_ref):
    width = normed.shape[-1]
    return rounded(matmul(normed, qkv_ref[:, :width])) * HEAD_SIZE**-0.5


def make_keys(normed, qkv_ref):
    width = normed.shape[-1]
    return matmul(normed, qkv_ref[:, width:])


def inner_kernel(
    own_w_ref,
    own_e_ref,
    west_ref,
    east_ref,
    gain_ref,
    qkv_ref,
    out_w_ref,
    out_ref,
    query_ref,
    state_ref,
):
    rows, width = own_w_ref.shape
    count = rows - 2 * RIM
    gain = gain_ref[...]
    own = jnp.concatenate([r[...].astype(jnp.float32) for r in (own_w_ref, own_e_ref)], axis=0)
    normed = layer_norm(own, gain)
    query = make_query(normed, qkv_ref)
    halos = jnp.concatenate([r[...].astype(jnp.float32) for r in (west_ref, east_ref)], axis=0)
    kv = make_keys(jnp.concatenate([normed, layer_norm(halos, gain)], axis=0), qkv_ref)
    mine, halos = kv[: 2 * rows], kv[2 * rows :]
    rim = level_bias(RIM, 2 * RIM)
    for edge in range(2):
        for side in range(2):
            place = edge * 2 + side
            begin = side * rows + edge * (rows - RIM)
            at = slice(begin, begin + RIM)
            query_ref[place] = query[at]
            both = jnp.concatenate([mine[at], halos[at]], axis=0).astype(jnp.bfloat16)
            for i, value in enumerate(attend(query[at], both, rim)):
                state_ref[i, place] = value
    bias = level_bias(count, 2 * count)
    states, tokens = [], []
    for side in range(2):
        at = slice(side * rows + RIM, (side + 1) * rows - RIM)
        both = jnp.concatenate([mine[at], halos[at]], axis=0).astype(jnp.bfloat16)
        states.append(attend(query[at], both, bias))
        tokens.append(own[at])
    mixed = project(jnp.concatenate(tokens, axis=0), states, out_w_ref)
    for side in range(2):
        place_half(out_ref, slice(None), side, mixed[side * count : (side + 1) * count])


def place_half(out_ref, at, side, half):
    half = half.reshape(-1, HALF, LEVELS, half.shape[-1]).astype(jnp.bfloat16)
    out_ref[at, side * HALF : (side + 1) * HALF] = half


def edge_kernel(
    closed_ref,
    query_ref,
    state_ref,
    north_ref,
    south_ref,
    own_w_ref,
    own_e_ref,
    middle_ref,
    gain_ref,
    qkv_ref,
    out_w_ref,
    out_ref,
):
    rows, width = own_w_ref.shape
    beyond = [r[part].astype(jnp.float32) for r in (north_ref, south_ref) for part in range(4)]
    beyond = make_keys(layer_norm(jnp.concatenate(beyond, axis=0), gain_ref[...]), qkv_ref).astype(jnp.bfloat16)
    levels = level_bias(RIM, 2 * RIM)
    own = [r[...].astype(jnp.float32) for r in (own_w_ref, own_e_ref)]
    states, tokens = [], []
    for edge in range(2):
        bias = levels + closed_ref[edge]
        for side in range(2):
            place = edge * 2 + side
            begin = edge * (rows - RIM)
            more = attend(query_ref[place], beyond[2 * place * RIM : 2 * (place + 1) * RIM], bias)
            states.append(add_keys(tuple(state_ref[i, place] for i in range(3)), more))
            tokens.append(own[side][begin : begin + RIM])
    mixed = project(jnp.concatenate(tokens, axis=0), states, out_w_ref)
    out_ref[EDGE : out_ref.shape[0] - EDGE] = middle_ref[...]
    for edge in range(2):
        at = slice(0, EDGE) if edge == 0 else slice(out_ref.shape[0] - EDGE, out_ref.shape[0])
        for side in range(2):
            place = edge * 2 + side
            place_half(out_ref, at, side, mixed[place * RIM : (place + 1) * RIM])


def call(kernel, results, flops, *operands):
    moved = sum(x.size * x.dtype.itemsize for x in (*operands, *results))
    specs = [pl.BlockSpec(memory_space=pltpu.SMEM if x.ndim == 1 else pltpu.VMEM) for x in operands]
    return pl.pallas_call(
        kernel,
        out_shape=results,
        in_specs=specs,
        out_specs=[pl.BlockSpec(memory_space=pltpu.VMEM)] * len(results),
        compiler_params=pltpu.CompilerParams(vmem_limit_bytes=14 * 2**20),
        cost_estimate=pl.CostEstimate(flops=flops, bytes_accessed=moved, transcendentals=0),
    )(*operands)


def shards(tokens, gain_attn, weight_qkv, weight_out):
    lev_count, row_count, col_count, width = tokens.shape
    rows = row_count * HALF * lev_count
    by_place = tokens.transpose(1, 2, 0, 3)
    own_w = by_place[:, :HALF].reshape(rows, width)
    own_e = by_place[:, HALF:].reshape(rows, width)
    east = shift(own_w, "lon", -1, True)
    west = shift(own_e, "lon", 1, True)

    first = jnp.zeros((4, RIM, width), tokens.dtype)
    last = first
    for part, half in ((0, own_w), (2, own_e), (1, west), (3, east)):
        first = lax.dynamic_update_slice(first, half[None, :RIM], (part, 0, 0))
        last = lax.dynamic_update_slice(last, half[None, rows - RIM :], (part, 0, 0))
    south = shift(first, "lat", -1, False)
    north = shift(last, "lat", 1, False)
    gain = gain_attn.reshape(1, width)
    place = lax.axis_index("lat")
    closed = jnp.stack([place == 0, place == lax.axis_size("lat") - 1])
    closed = jnp.where(closed, FAR, 0.0).astype(jnp.float32)

    def shape(*dims, dtype=jnp.float32):
        return jax.ShapeDtypeStruct(dims, dtype)

    middle, query, state = call(
        inner_kernel,
        [
            shape(row_count - 2 * EDGE, col_count, lev_count, width, dtype=jnp.bfloat16),
            shape(4, RIM, width),
            shape(3, 4, RIM, width),
        ],
        2_500_000_000,
        own_w,
        own_e,
        west,
        east,
        gain,
        weight_qkv,
        weight_out,
    )
    (mixed,) = call(
        edge_kernel,
        [shape(row_count, col_count, lev_count, width, dtype=jnp.bfloat16)],
        1_000_000_000,
        closed,
        query,
        state,
        north,
        south,
        own_w,
        own_e,
        middle,
        gain,
        weight_qkv,
        weight_out,
    )
    return mixed.transpose(2, 0, 1, 3)


def solution(mesh):
    placed = (P(None, "lat", "lon", None), P(), P(), P())
    return jax.shard_map(
        shards, mesh=mesh, in_specs=placed, out_specs=P(None, "lat", "lon", None), check_vma=False
    )
```

```python
import jax
import jax.numpy as jnp
from jax import lax
from jax.experimental import pallas as pl
from jax.experimental.pallas import tpu as pltpu
from jax.sharding import PartitionSpec as P

HEADS = 8
HEAD_SIZE = 64
GROUP = 4
SPAN = GROUP * HEAD_SIZE
EPS = 1e-05
FAR = -1e30
HALF = 6
EDGE = 3
LEVELS = 4
RIM = EDGE * HALF * LEVELS


def shift(value, axis, by, wrap):
    count = lax.axis_size(axis)
    pairs = [(i, (i + by) % count) for i in range(count) if wrap or 0 <= i + by < count]
    return lax.ppermute(value, axis, pairs)


def layer_norm(values, gain):
    center = values - jnp.mean(values, axis=-1, keepdims=True)
    spread = jnp.mean(center * center, axis=-1, keepdims=True)
    return (center * lax.rsqrt(spread + EPS) * gain).astype(jnp.bfloat16)


def matmul(a, b):
    return jnp.dot(a, b, preferred_element_type=jnp.float32)


def rounded(values):
    return values.astype(jnp.bfloat16).astype(jnp.float32)


def level_bias(rows, keys):
    def part(axis):
        level = lax.broadcasted_iota(jnp.int32, (rows, keys), axis) & (LEVELS - 1)
        return jnp.where(level == 0, 2, jnp.where(level == LEVELS - 1, 1, 0))

    return jnp.where(part(0) == part(1), 0.0, FAR).astype(jnp.float32)


def attend(query, kv, bias):
    rows, width = query.shape
    owner = lax.broadcasted_iota(jnp.int32, (rows, SPAN), 1) >> 6
    tall = jnp.concatenate([bias] * GROUP, axis=0)

    def merge(values):
        merged = jnp.broadcast_to(values[:rows], (rows, SPAN))
        for h in range(1, GROUP):
            merged = jnp.where(owner == h, values[h * rows : (h + 1) * rows], merged)
        return merged

    parts = []
    for start in range(0, width, SPAN):
        piece = query[:, start : start + SPAN]
        spread = jnp.concatenate(
            [jnp.where(owner == h, piece, 0.0) for h in range(GROUP)], axis=0
        ).astype(jnp.bfloat16)
        scores = lax.dot_general(
            spread,
            kv[:, start : start + SPAN],
            (((1,), (1,)), ((), ())),
            preferred_element_type=jnp.float32,
        )
        scores = scores + tall
        top = jnp.max(scores, axis=-1, keepdims=True)
        expo = jnp.exp(scores - top)
        total = jnp.sum(expo, axis=-1, keepdims=True)
        out = matmul(expo.astype(jnp.bfloat16), kv[:, width + start : width + start + SPAN])
        parts.append((merge(out), merge(top), merge(total)))
    return tuple(jnp.concatenate(p, axis=1) for p in zip(*parts))


def add_keys(state, more):
    out, top, total = state
    out_2, top_2, total_2 = more
    peak = jnp.maximum(top, top_2)
    old, new = jnp.exp(top - peak), jnp.exp(top_2 - peak)
    return out * old + out_2 * new, peak, total * old + total_2 * new


def project(tokens, states, weight_ref):
    heads = [out * (1.0 / total) for out, _, total in states]
    branch = matmul(jnp.concatenate(heads, axis=0).astype(jnp.bfloat16), weight_ref[...])
    return tokens + rounded(branch)


def make_query(normed, qkv_ref):
    width = normed.shape[-1]
    return rounded(matmul(normed, qkv_ref[:, :width])) * HEAD_SIZE**-0.5


def make_keys(normed, qkv_ref):
    width = normed.shape[-1]
    return matmul(normed, qkv_ref[:, width:])


def inner_kernel(
    own_w_ref,
    own_e_ref,
    west_ref,
    east_ref,
    gain_ref,
    qkv_ref,
    out_w_ref,
    out_ref,
    query_ref,
    state_ref,
):
    rows, width = own_w_ref.shape
    count = rows - 2 * RIM
    gain = gain_ref[...]
    own = jnp.concatenate([r[...].astype(jnp.float32) for r in (own_w_ref, own_e_ref)], axis=0)
    normed = layer_norm(own, gain)
    query = make_query(normed, qkv_ref)
    halos = jnp.concatenate([r[...].astype(jnp.float32) for r in (west_ref, east_ref)], axis=0)
    kv = make_keys(jnp.concatenate([normed, layer_norm(halos, gain)], axis=0), qkv_ref)
    mine, halos = kv[: 2 * rows], kv[2 * rows :]
    rim = level_bias(RIM, 2 * RIM)
    for edge in range(2):
        for side in range(2):
            place = edge * 2 + side
            begin = side * rows + edge * (rows - RIM)
            at = slice(begin, begin + RIM)
            query_ref[place] = query[at]
            both = jnp.concatenate([mine[at], halos[at]], axis=0).astype(jnp.bfloat16)
            for i, value in enumerate(attend(query[at], both, rim)):
                state_ref[i, place] = value
    bias = level_bias(count, 2 * count)
    states, tokens = [], []
    for side in range(2):
        at = slice(side * rows + RIM, (side + 1) * rows - RIM)
        both = jnp.concatenate([mine[at], halos[at]], axis=0).astype(jnp.bfloat16)
        states.append(attend(query[at], both, bias))
        tokens.append(own[at])
    mixed = project(jnp.concatenate(tokens, axis=0), states, out_w_ref)
    for side in range(2):
        place_half(out_ref, slice(None), side, mixed[side * count : (side + 1) * count])


def place_half(out_ref, at, side, half):
    half = half.reshape(-1, HALF, LEVELS, half.shape[-1]).astype(jnp.bfloat16)
    out_ref[at, side * HALF : (side + 1) * HALF] = half


def edge_kernel(
    closed_ref,
    query_ref,
    state_ref,
    north_ref,
    south_ref,
    far_north_ref,
    far_south_ref,
    own_w_ref,
    own_e_ref,
    middle_ref,
    gain_ref,
    qkv_ref,
    out_w_ref,
    out_ref,
):
    rows, width = own_w_ref.shape
    refs = ((north_ref, far_north_ref), (south_ref, far_south_ref))
    beyond = [r[side].astype(jnp.float32) for pair in refs for side in range(2) for r in pair]
    beyond = make_keys(layer_norm(jnp.concatenate(beyond, axis=0), gain_ref[...]), qkv_ref).astype(jnp.bfloat16)
    levels = level_bias(RIM, 2 * RIM)
    own = [r[...].astype(jnp.float32) for r in (own_w_ref, own_e_ref)]
    states, tokens = [], []
    for edge in range(2):
        bias = levels + closed_ref[edge]
        for side in range(2):
            place = edge * 2 + side
            begin = edge * (rows - RIM)
            more = attend(query_ref[place], beyond[2 * place * RIM : 2 * (place + 1) * RIM], bias)
            states.append(add_keys(tuple(state_ref[i, place] for i in range(3)), more))
            tokens.append(own[side][begin : begin + RIM])
    mixed = project(jnp.concatenate(tokens, axis=0), states, out_w_ref)
    out_ref[EDGE : out_ref.shape[0] - EDGE] = middle_ref[...]
    for edge in range(2):
        at = slice(0, EDGE) if edge == 0 else slice(out_ref.shape[0] - EDGE, out_ref.shape[0])
        for side in range(2):
            place = edge * 2 + side
            place_half(out_ref, at, side, mixed[place * RIM : (place + 1) * RIM])


def call(kernel, results, flops, *operands):
    moved = sum(x.size * x.dtype.itemsize for x in (*operands, *results))
    specs = [pl.BlockSpec(memory_space=pltpu.SMEM if x.ndim == 1 else pltpu.VMEM) for x in operands]
    return pl.pallas_call(
        kernel,
        out_shape=results,
        in_specs=specs,
        out_specs=[pl.BlockSpec(memory_space=pltpu.VMEM)] * len(results),
        compiler_params=pltpu.CompilerParams(vmem_limit_bytes=14 * 2**20),
        cost_estimate=pl.CostEstimate(flops=flops, bytes_accessed=moved, transcendentals=0),
    )(*operands)


def shards(tokens, gain_attn, weight_qkv, weight_out):
    lev_count, row_count, col_count, width = tokens.shape
    rows = row_count * HALF * lev_count
    by_place = tokens.transpose(1, 2, 0, 3)
    own_w = by_place[:, :HALF].reshape(rows, width)
    own_e = by_place[:, HALF:].reshape(rows, width)
    east = shift(own_w, "lon", -1, True)
    west = shift(own_e, "lon", 1, True)

    def rim(*halves):
        return jnp.stack([h[:RIM] for h in halves]), jnp.stack([h[rows - RIM :] for h in halves])

    first, last = rim(own_w, own_e)
    south = shift(first, "lat", -1, False)
    north = shift(last, "lat", 1, False)
    first, last = rim(west, east)
    far_south = shift(first, "lat", -1, False)
    far_north = shift(last, "lat", 1, False)
    gain = gain_attn.reshape(1, width)
    place = lax.axis_index("lat")
    closed = jnp.stack([place == 0, place == lax.axis_size("lat") - 1])
    closed = jnp.where(closed, FAR, 0.0).astype(jnp.float32)

    def shape(*dims, dtype=jnp.float32):
        return jax.ShapeDtypeStruct(dims, dtype)

    middle, query, state = call(
        inner_kernel,
        [
            shape(row_count - 2 * EDGE, col_count, lev_count, width, dtype=jnp.bfloat16),
            shape(4, RIM, width),
            shape(3, 4, RIM, width),
        ],
        2_500_000_000,
        own_w,
        own_e,
        west,
        east,
        gain,
        weight_qkv,
        weight_out,
    )
    (mixed,) = call(
        edge_kernel,
        [shape(row_count, col_count, lev_count, width, dtype=jnp.bfloat16)],
        1_000_000_000,
        closed,
        query,
        state,
        north,
        south,
        far_north,
        far_south,
        own_w,
        own_e,
        middle,
        gain,
        weight_qkv,
        weight_out,
    )
    return mixed.transpose(2, 0, 1, 3)


def solution(mesh):
    placed = (P(None, "lat", "lon", None), P(), P(), P())
    return jax.shard_map(
        shards, mesh=mesh, in_specs=placed, out_specs=P(None, "lat", "lon", None), check_vma=False
    )
```
